32 devices in a mesh: seq: 16 (over z, y, x), head: 2 (over core).
Axes of the slice: x: 2, y: 2, z: 4, core: 2. Of those that a mesh axis runs over, the one named last changes fastest.
Arguments:
- queries: bfloat16 [4096, 1024], P('seq', 'head'), may hold values from -6 to 6
- key_rows: bfloat16 [4096, 1024], P('seq', 'head'), may hold values from -6 to 6
- values: bfloat16 [4096, 1024], P('seq', 'head'), may hold values from -12 to 12
- cotangent: bfloat16 [4096, 1024], P('seq', 'head'), may hold values from -12 to 12
- carried_state: float32 [8, 128, 128], P('head'), may hold values from -192 to 192
- norm_gain: float32 [1024], P('head'), may hold values from 0.25 to 1.75
Outputs:
- attended: bfloat16 [4096, 1024], P('seq', 'head')
- gradient_queries: bfloat16 [4096, 1024], P('seq', 'head')
- gradient_keys: bfloat16 [4096, 1024], P('seq', 'head')
- grad_value: bfloat16 [4096, 1024], P('seq', 'head')
- grad_state: float32 [8, 128, 128], P('head')
- grad_gain: float32 [1024], P('head')
The draws below stay inside these ranges and needn't reach their ends.
All inputs are finite; a program needn't handle non-finite values.
Results may differ from the reference program's by a relative error of at most 0.0065.
Values may be sent and summed in bfloat16 or wider, within the bound.
No kernel may reach another device: no remote copies, remote signals or barrier semaphores. Data moves between devices by JAX's collectives and lax.ppermute only.
A program may use at most 64 MiB of HBM per device.

```python
import jax
import jax.numpy as jnp
from jax import lax

DH = 128
TOK_DEV = 256
HEADS = 8
F = 1024
TOKENS = 4096


def draw_values(key, part):
    columns = jnp.arange(HEADS * DH)
    position = (columns // DH).astype(jnp.float32) / max(HEADS - 1, 1)
    noise = jnp.clip(jax.random.normal(key, (TOKENS, HEADS * DH), jnp.float32), -6.0, 6.0)
    factor = 0.6 * jnp.power(3.0, position)
    return (noise * factor[None, :]).astype(jnp.bfloat16)


def draw_cotangent(key, part):
    first = jax.random.fold_in(key, 0)
    position = jnp.arange(TOKENS).astype(jnp.float32) / max(TOKENS - 1, 1)
    noise = jnp.clip(jax.random.normal(first, (TOKENS, HEADS * DH), jnp.float32), -6.0, 6.0)
    factor = 0.6 * jnp.power(3.0, position)
    result = noise * factor[:, None]
    return result.astype(jnp.bfloat16)


def shard_levels(own_key, shape, pieces, least, top_value):
    level = 1.0
    for dim, blocks in pieces:
        draws = jax.random.uniform(jax.random.fold_in(jax.random.fold_in(own_key, 6), dim), (blocks,), jnp.float32, least / len(pieces), top_value / len(pieces))
        level = level * jnp.repeat(jnp.exp(draws), shape[dim] // blocks).reshape((-1,) + (1,) * (len(shape) - 1 - dim))
    return level


def bell_draw(own_key, dims, scale, limit, cuts=(), held_as=jnp.bfloat16):
    drawn = jax.random.normal(own_key, dims, jnp.float32) * scale
    if len(cuts) > 0:
        drawn = shard_levels(own_key, dims, cuts, -0.22, 0.18) * drawn
    return jnp.clip(drawn, min=-limit, max=limit).astype(held_as)


def setup_inputs(seed: int = 0) -> dict:
    arg_keys = jax.random.split(jax.random.key(seed), 7)
    queries = bell_draw(arg_keys[0], (TOKENS, F), 1.0, 6.0, ((0, 16), (1, 2)))
    key_rows = bell_draw(arg_keys[1], (TOKENS, F), 1.0, 6.0, ((0, 16), (1, 2)))
    values = draw_values(jax.random.fold_in(arg_keys[6], 71), 0)
    cotangent = draw_cotangent(jax.random.fold_in(arg_keys[6], 71), 0)
    carried_state = bell_draw(arg_keys[4], (HEADS, DH, DH), (TOK_DEV // 8), 192.0, ((0, 2),), jnp.float32)
    norm_gain = jnp.clip(1.0 + 0.15 * jax.random.normal(arg_keys[5], (F,), jnp.float32), 0.25, 1.75)
    return dict(queries=queries, key_rows=key_rows, values=values, cotangent=cotangent, carried_state=carried_state, norm_gain=norm_gain)


EPS = 1e-05

def inner_product(form, left, right):
    return jnp.einsum(form, left.astype(jnp.float32), right.astype(jnp.float32), precision=lax.Precision.HIGHEST)

def reference(queries, key_rows, values, cotangent, carried_state, norm_gain):
    blocks = TOKENS // TOK_DEV
    width = HEADS * DH

    def split(rows):
        return rows.reshape(blocks, TOK_DEV, HEADS, DH)
    causal_mask = jnp.arange(TOK_DEV)[:, None] >= jnp.arange(TOK_DEV)[None, :]
    gain_heads = norm_gain.astype(jnp.float32).reshape(HEADS, DH)

    def forward_block(prefix, inputs):
        block_queries, block_keys, block_values, cot_b = inputs
        preceding_part = prefix.astype(jnp.bfloat16)
        score_matrix = jnp.where(causal_mask, inner_product('ftz,ytz->tfy', block_queries, block_keys), jnp.float32(0.0)).astype(jnp.bfloat16)
        unnormed = inner_product('hlm,mhe->lhe', score_matrix, block_values) + inner_product('lhd,hde->lhe', block_queries, preceding_part)
        square_sum = lax.optimization_barrier(jnp.sum(unnormed * unnormed, axis=(1, 2)))
        norm_scale = jnp.sqrt(square_sum / width + EPS)[:, None, None]
        normed = unnormed / norm_scale
        attended = (gain_heads * normed).astype(jnp.bfloat16)
        cot_wide = cot_b.astype(jnp.float32)
        scaled = cot_wide * gain_heads
        dot_sum = lax.optimization_barrier(jnp.sum(scaled * unnormed, axis=(1, 2)))[:, None, None]
        grad_unnormed = ((scaled - normed * (dot_sum / (width * norm_scale))) / norm_scale).astype(jnp.bfloat16)
        gain_term = lax.optimization_barrier(jnp.sum(cot_wide * normed, axis=0))
        grad_group = inner_product('lhd,lhe->hde', block_queries, grad_unnormed)
        group_state = inner_product('lhd,lhe->hde', block_keys, block_values)
        return (prefix + group_state, (prefix, attended, grad_unnormed, gain_term, grad_group))
    inputs = (split(queries), split(key_rows), split(values), split(cotangent))
    unused, outputs = lax.scan(forward_block, carried_state.astype(jnp.float32), inputs)
    prefixes, attended, grad_unnormed, gain_terms, grad_groups = outputs
    grad_state = lax.optimization_barrier(jnp.sum(grad_groups, axis=0))
    inclusive = lax.cumsum(grad_groups, axis=0, reverse=True)
    suffixes = jnp.concatenate([inclusive[1:], jnp.zeros_like(inclusive[:1])], axis=0)

    def backward_block(items):
        block_queries, block_keys, block_values, block_gradient, prefix, suffix = items
        preceding_part = prefix.astype(jnp.bfloat16)
        following_part = suffix.astype(jnp.bfloat16)
        score_matrix = jnp.where(causal_mask, inner_product('ftz,ytz->tfy', block_queries, block_keys), jnp.float32(0.0)).astype(jnp.bfloat16)
        blended_output = jnp.where(causal_mask, inner_product('lhe,mhe->hlm', block_gradient, block_values), jnp.float32(0.0)).astype(jnp.bfloat16)
        query_gradient = inner_product('krx,xkn->rkn', blended_output, block_keys) + inner_product('xif,iuf->xiu', block_gradient, preceding_part)
        key_gradient = inner_product('nox,ony->xny', blended_output, block_queries) + inner_product('yon,otn->yot', block_values, following_part)
        value_gradient = inner_product('nou,onk->unk', score_matrix, block_gradient) + inner_product('klj,ljr->klr', block_keys, following_part)
        return (query_gradient.astype(jnp.bfloat16), key_gradient.astype(jnp.bfloat16), value_gradient.astype(jnp.bfloat16))
    query_gradient, key_gradient, value_gradient = lax.map(backward_block, (inputs[0], inputs[1], inputs[2], grad_unnormed, prefixes, suffixes))
    grad_gain = lax.optimization_barrier(jnp.sum(gain_terms, axis=0)).reshape(width)
    return (attended.reshape(TOKENS, width), query_gradient.reshape(TOKENS, width), key_gradient.reshape(TOKENS, width), value_gradient.reshape(TOKENS, width), grad_state, grad_gain)
```

```python
import functools

import jax
import jax.numpy as jnp
from jax import lax
from jax.experimental import pallas as pl
from jax.experimental.pallas import tpu as pltpu
from jax.sharding import PartitionSpec as P

EPS = 1e-05
F32 = jnp.float32
BF16 = jnp.bfloat16


def dot(a, b, ca, cb):
    return lax.dot_general(a, b, (((ca,), (cb,)), ((), ())), preferred_element_type=F32)


def call(kernel, outs, flops, nbytes):
    return pl.pallas_call(
        kernel,
        out_shape=outs,
        cost_estimate=pl.CostEstimate(flops=flops, bytes_accessed=nbytes, transcendentals=0),
    )


def cols(h, dim):
    return slice(h * dim, (h + 1) * dim)


def state_kernel(heads, dim, k_ref, v_ref, out_ref):
    for h in range(heads):
        c = cols(h, dim)
        out_ref[c, :] = dot(k_ref[:, c], v_ref[:, c], 0, 0).astype(BF16)


def causal(length):
    rows = lax.broadcasted_iota(jnp.int32, (length, length), 0)
    return rows >= lax.broadcasted_iota(jnp.int32, (length, length), 1)


def scores_kernel(heads, dim, q_ref, k_ref, v_ref, local_ref):
    mask = causal(q_ref.shape[0])
    for h in range(heads):
        c = cols(h, dim)
        scores = jnp.where(mask, dot(q_ref[:, c], k_ref[:, c], 1, 1), 0.0).astype(BF16)
        local_ref[:, c] = dot(scores, v_ref[:, c], 1, 0)


def gathered(parts, rows, reverse):
    mine = lax.axis_index("seq")
    total = None
    for bit, part in enumerate(parts):
        reached = ((mine >> bit) & 1) == (0 if reverse else 1)
        term = jnp.where(reached, part[rows, :].astype(F32), 0.0)
        total = term if total is None else total + term
    return total


def unnormed_kernel(heads, dim, rounds, *refs):
    parts = refs[:rounds]
    q_ref, local_ref, cot_ref, carried_ref, gain_ref = refs[rounds : rounds + 5]
    un_ref, prefix_ref, sums_ref = refs[rounds + 5 :]
    square = None
    for h in range(heads):
        c = cols(h, dim)
        prefix = carried_ref[h]
        if parts:
            prefix = prefix + gathered(parts, c, False)
        prefix = prefix.astype(BF16)
        prefix_ref[c, :] = prefix
        un = local_ref[:, c] + dot(q_ref[:, c], prefix, 1, 0)
        un_ref[:, c] = un
        scaled = cot_ref[:, c].astype(F32) * gain_ref[:, c]
        square = un * un if square is None else square + un * un
        product = scaled * un if h == 0 else product + scaled * un
    square = jnp.sum(square, axis=1, keepdims=True)
    product = jnp.sum(product, axis=1, keepdims=True)
    lane = lax.broadcasted_iota(jnp.int32, sums_ref.shape, 1)
    sums_ref[...] = jnp.where(lane < sums_ref.shape[1] // 2, square, product)


def norm_kernel(heads, dim, width, sums_ref, other_ref, un_ref, cot_ref, gain_ref, q_ref, att_ref, gun_ref, msg_ref):
    sums = sums_ref[...] + other_ref[...]
    half = sums.shape[1] // 2
    inverse = 1.0 / jnp.sqrt(sums[:, 0:1] / width + EPS)
    factor = (sums[:, half : half + 1] * inverse) / width * inverse * inverse
    for h in range(heads):
        c = cols(h, dim)
        un = un_ref[:, c]
        cot = cot_ref[:, c].astype(F32)
        gain = gain_ref[:, c]
        normed = un * inverse
        att_ref[:, c] = (gain * normed).astype(BF16)
        gun = (cot * gain * inverse - un * factor).astype(BF16)
        gun_ref[:, c] = gun
        msg_ref[c, :] = dot(q_ref[:, c], gun, 0, 0).astype(BF16)
        row = heads * dim + h
        msg_ref[row : row + 1, :] = jnp.sum(cot * normed, axis=0, keepdims=True).astype(BF16)
    rest = heads * dim + heads
    msg_ref[rest:, :] = jnp.zeros((msg_ref.shape[0] - rest, dim), BF16)


def local_grad_kernel(heads, dim, q_ref, k_ref, v_ref, gun_ref, prefix_ref, gq_ref, gk_ref, gv_ref):
    mask = causal(q_ref.shape[0])
    for h in range(heads):
        c = cols(h, dim)
        q, k, v, gun = q_ref[:, c], k_ref[:, c], v_ref[:, c], gun_ref[:, c]
        mixed = jnp.where(mask, dot(gun, v, 1, 1), 0.0).astype(BF16)
        scores = jnp.where(mask, dot(q, k, 1, 1), 0.0).astype(BF16)
        gq_ref[:, c] = (dot(mixed, k, 1, 0) + dot(gun, prefix_ref[c, :], 1, 1)).astype(BF16)
        gk_ref[:, c] = dot(mixed, q, 0, 0)
        gv_ref[:, c] = dot(scores, gun, 0, 0)


def final_kernel(heads, dim, rounds, *refs):
    parts = refs[:rounds]
    total_ref, k_ref, v_ref, gk_ref, gv_ref = refs[rounds : rounds + 5]
    gk_out, gv_out, state_out, gain_out = refs[rounds + 5 :]
    for h in range(heads):
        c = cols(h, dim)
        total = total_ref[c, :].astype(F32)
        gk, gv = gk_ref[:, c], gv_ref[:, c]
        row = slice(heads * dim + h, heads * dim + h + 1)
        gain = total_ref[row, :].astype(F32)
        if parts:
            suffix = gathered(parts, c, True).astype(BF16)
            gk = gk + dot(v_ref[:, c], suffix, 1, 1)
            gv = gv + dot(k_ref[:, c], suffix, 1, 0)
            total = total + parts[-1][c, :].astype(F32)
            gain = gain + parts[-1][row, :].astype(F32)
        gk_out[:, c] = gk.astype(BF16)
        gv_out[:, c] = gv.astype(BF16)
        state_out[h] = total
        gain_out[:, c] = gain


def exchange(message, count):
    received = []
    distance = 1
    while distance < count:
        if received:
            message = message + received[-1]
        pairs = [(i, i ^ distance) for i in range(count)]
        received.append(lax.ppermute(message, "seq", pairs))
        distance *= 2
    return message, received


def on_device(queries, key_rows, values, cotangent, carried_state, norm_gain):
    length, width = queries.shape
    heads, dim = carried_state.shape[:2]
    count = lax.axis_size("seq")
    head_count = lax.axis_size("head")
    assert count & (count - 1) == 0
    assert width == heads * dim
    total_width = width * head_count
    gain = norm_gain.reshape(1, width)
    shape = jax.ShapeDtypeStruct
    tokens_bf = shape((length, width), BF16)
    tokens_f32 = shape((length, width), F32)
    block = 2 * length * dim * dim * heads
    square = 2 * length * length * dim * heads
    size = length * width * 2
    state_size = heads * dim * dim * 2

    state = call(
        functools.partial(state_kernel, heads, dim),
        shape((heads * dim, dim), BF16), block, 2 * size + state_size,
    )(key_rows, values)
    _, received = exchange(state, count)
    local = call(
        functools.partial(scores_kernel, heads, dim), tokens_f32, 2 * square, 5 * size,
    )(queries, key_rows, values)
    rounds = len(received)
    unnormed, prefix, sums = call(
        functools.partial(unnormed_kernel, heads, dim, rounds),
        (tokens_f32, shape((heads * dim, dim), BF16), shape((length, 128), F32)),
        block, 6 * size + (rounds + 3) * state_size,
    )(*received, queries, local, cotangent, carried_state, gain)
    other = jnp.zeros_like(sums)
    partner = sums
    for step in range(1, head_count):
        partner = lax.ppermute(partner, "head", [(i, (i + 1) % head_count) for i in range(head_count)])
        other = other + partner if step > 1 else partner
    rows = heads * dim + -(-heads // 16) * 16
    attended, grad_unnormed, message = call(
        functools.partial(norm_kernel, heads, dim, total_width),
        (tokens_bf, tokens_bf, shape((rows, dim), BF16)), block, 6 * size + state_size,
    )(sums, other, unnormed, cotangent, gain, queries)
    message, received = exchange(message, count)
    grad_q, local_k, local_v = call(
        functools.partial(local_grad_kernel, heads, dim),
        (tokens_bf, tokens_f32, tokens_f32), 5 * square + block, 9 * size + state_size,
    )(queries, key_rows, values, grad_unnormed, prefix)
    grad_k, grad_v, grad_state, grad_gain = call(
        functools.partial(final_kernel, heads, dim, rounds),
        (tokens_bf, tokens_bf, shape((heads, dim, dim), F32), shape((1, width), F32)),
        2 * block, 8 * size + (rounds + 2) * state_size,
    )(*received, message, key_rows, values, local_k, local_v)
    return attended, grad_q, grad_k, grad_v, grad_state, grad_gain.reshape(width)


def solution(mesh):
    tokens = P("seq", "head")
    specs = (P("head", None, None), P("head"))
    return jax.shard_map(
        on_device,
        mesh=mesh,
        in_specs=(tokens,) * 4 + specs,
        out_specs=(tokens,) * 4 + specs,
        check_vma=False,
    )
```

```python
import functools

import jax
import jax.numpy as jnp
from jax import lax
from jax.experimental import pallas as pl
from jax.experimental.pallas import tpu as pltpu
from jax.sharding import PartitionSpec as P

EPS = 1e-05
F32 = jnp.float32
BF16 = jnp.bfloat16
VMEM = 16 * 2**20


def dot(a, b, ca, cb):
    return lax.dot_general(a, b, (((ca,), (cb,)), ((), ())), preferred_element_type=F32)


def call(kernel, outs, flops, nbytes):
    return pl.pallas_call(
        kernel,
        out_shape=outs,
        compiler_params=pltpu.CompilerParams(vmem_limit_bytes=VMEM),
        cost_estimate=pl.CostEstimate(flops=flops, bytes_accessed=nbytes, transcendentals=0),
    )


def cols(h, dim):
    return slice(h * dim, (h + 1) * dim)


def state_kernel(heads, dim, k_ref, v_ref, out_ref):
    for h in range(heads):
        c = cols(h, dim)
        out_ref[c, :] = dot(k_ref[:, c], v_ref[:, c], 0, 0).astype(BF16)


def causal(length):
    rows = lax.broadcasted_iota(jnp.int32, (length, length), 0)
    return rows >= lax.broadcasted_iota(jnp.int32, (length, length), 1)


def scores_kernel(heads, dim, q_ref, k_ref, v_ref, local_ref):
    mask = causal(q_ref.shape[0])
    for h in range(heads):
        c = cols(h, dim)
        scores = jnp.where(mask, dot(q_ref[:, c], k_ref[:, c], 1, 1), 0.0).astype(BF16)
        local_ref[:, c] = dot(scores, v_ref[:, c], 1, 0)


def gathered(parts, rows, reverse):
    mine = lax.axis_index("seq")
    total = None
    for bit, part in enumerate(parts):
        reached = ((mine >> bit) & 1) == (0 if reverse else 1)
        term = jnp.where(reached, part[rows, :].astype(F32), 0.0)
        total = term if total is None else total + term
    return total


def unnormed_kernel(heads, dim, rounds, *refs):
    parts = refs[:rounds]
    q_ref, local_ref, cot_ref, carried_ref, gain_ref = refs[rounds : rounds + 5]
    un_ref, prefix_ref, sums_ref = refs[rounds + 5 :]
    square = None
    for h in range(heads):
        c = cols(h, dim)
        prefix = carried_ref[h]
        if parts:
            prefix = prefix + gathered(parts, c, False)
        prefix = prefix.astype(BF16)
        prefix_ref[c, :] = prefix
        un = local_ref[:, c] + dot(q_ref[:, c], prefix, 1, 0)
        un_ref[:, c] = un
        scaled = cot_ref[:, c].astype(F32) * gain_ref[:, c]
        square = un * un if square is None else square + un * un
        product = scaled * un if h == 0 else product + scaled * un
    square = jnp.sum(square, axis=1, keepdims=True)
    product = jnp.sum(product, axis=1, keepdims=True)
    lane = lax.broadcasted_iota(jnp.int32, sums_ref.shape, 1)
    sums_ref[...] = jnp.where(lane < sums_ref.shape[1] // 2, square, product)


def norm_kernel(heads, dim, width, sums_ref, other_ref, un_ref, cot_ref, gain_ref, q_ref, att_ref, gun_ref, msg_ref):
    sums = sums_ref[...] + other_ref[...]
    half = sums.shape[1] // 2
    inverse = 1.0 / jnp.sqrt(sums[:, 0:1] / width + EPS)
    factor = (sums[:, half : half + 1] * inverse) / width * inverse * inverse
    for h in range(heads):
        c = cols(h, dim)
        un = un_ref[:, c]
        cot = cot_ref[:, c].astype(F32)
        gain = gain_ref[:, c]
        normed = un * inverse
        att_ref[:, c] = (gain * normed).astype(BF16)
        gun = (cot * gain * inverse - un * factor).astype(BF16)
        gun_ref[:, c] = gun
        msg_ref[c, :] = dot(q_ref[:, c], gun, 0, 0).astype(BF16)
        row = heads * dim + h
        msg_ref[row : row + 1, :] = jnp.sum(cot * normed, axis=0, keepdims=True).astype(BF16)
    rest = heads * dim + heads
    msg_ref[rest:, :] = jnp.zeros((msg_ref.shape[0] - rest, dim), BF16)


def local_grad_kernel(heads, dim, q_ref, k_ref, v_ref, gun_ref, prefix_ref, gq_ref, gk_ref, gv_ref):
    mask = causal(q_ref.shape[0])
    for h in range(heads):
        c = cols(h, dim)
        q, k, v, gun = q_ref[:, c], k_ref[:, c], v_ref[:, c], gun_ref[:, c]
        mixed = jnp.where(mask, dot(gun, v, 1, 1), 0.0).astype(BF16)
        scores = jnp.where(mask, dot(q, k, 1, 1), 0.0).astype(BF16)
        gq_ref[:, c] = (dot(mixed, k, 1, 0) + dot(gun, prefix_ref[c, :], 1, 1)).astype(BF16)
        gk_ref[:, c] = dot(mixed, q, 0, 0)
        gv_ref[:, c] = dot(scores, gun, 0, 0)


def final_kernel(heads, dim, rounds, *refs):
    parts = refs[:rounds]
    total_ref, k_ref, v_ref, gk_ref, gv_ref = refs[rounds : rounds + 5]
    gk_out, gv_out, state_out, gain_out = refs[rounds + 5 :]
    for h in range(heads):
        c = cols(h, dim)
        total = total_ref[c, :].astype(F32)
        gk, gv = gk_ref[:, c], gv_ref[:, c]
        row = slice(heads * dim + h, heads * dim + h + 1)
        gain = total_ref[row, :].astype(F32)
        if parts:
            suffix = gathered(parts, c, True).astype(BF16)
            gk = gk + dot(v_ref[:, c], suffix, 1, 1)
            gv = gv + dot(k_ref[:, c], suffix, 1, 0)
            total = total + parts[-1][c, :].astype(F32)
            gain = gain + parts[-1][row, :].astype(F32)
        gk_out[:, c] = gk.astype(BF16)
        gv_out[:, c] = gv.astype(BF16)
        state_out[h] = total
        gain_out[:, c] = gain


def exchange(message, count):
    received = []
    distance = 1
    while distance < count:
        if received:
            message = message + received[-1]
        pairs = [(i, i ^ distance) for i in range(count)]
        received.append(lax.ppermute(message, "seq", pairs))
        distance *= 2
    return message, received


def on_device(queries, key_rows, values, cotangent, carried_state, norm_gain):
    length, width = queries.shape
    heads, dim = carried_state.shape[:2]
    count = lax.axis_size("seq")
    head_count = lax.axis_size("head")
    assert count & (count - 1) == 0
    assert width == heads * dim
    total_width = width * head_count
    gain = norm_gain.reshape(1, width)
    shape = jax.ShapeDtypeStruct
    tokens_bf = shape((length, width), BF16)
    tokens_f32 = shape((length, width), F32)
    block = 2 * length * dim * dim * heads
    square = 2 * length * length * dim * heads
    size = length * width * 2
    state_size = heads * dim * dim * 2

    state = call(
        functools.partial(state_kernel, heads, dim),
        shape((heads * dim, dim), BF16), block, 2 * size + state_size,
    )(key_rows, values)
    _, received = exchange(state, count)
    local = call(
        functools.partial(scores_kernel, heads, dim), tokens_f32, 2 * square, 5 * size,
    )(queries, key_rows, values)
    rounds = len(received)
    unnormed, prefix, sums = call(
        functools.partial(unnormed_kernel, heads, dim, rounds),
        (tokens_f32, shape((heads * dim, dim), BF16), shape((length, 128), F32)),
        block, 6 * size + (rounds + 3) * state_size,
    )(*received, queries, local, cotangent, carried_state, gain)
    other = jnp.zeros_like(sums)
    partner = sums
    for step in range(1, head_count):
        partner = lax.ppermute(partner, "head", [(i, (i + 1) % head_count) for i in range(head_count)])
        other = other + partner if step > 1 else partner
    rows = heads * dim + -(-heads // 16) * 16
    attended, grad_unnormed, message = call(
        functools.partial(norm_kernel, heads, dim, total_width),
        (tokens_bf, tokens_bf, shape((rows, dim), BF16)), block, 6 * size + state_size,
    )(sums, other, unnormed, cotangent, gain, queries)
    message, received = exchange(message, count)
    grad_q, local_k, local_v = call(
        functools.partial(local_grad_kernel, heads, dim),
        (tokens_bf, tokens_f32, tokens_f32), 5 * square + block, 9 * size + state_size,
    )(queries, key_rows, values, grad_unnormed, prefix)
    grad_k, grad_v, grad_state, grad_gain = call(
        functools.partial(final_kernel, heads, dim, rounds),
        (tokens_bf, tokens_bf, shape((heads, dim, dim), F32), shape((1, width), F32)),
        2 * block, 8 * size + (rounds + 2) * state_size,
    )(*received, message, key_rows, values, local_k, local_v)
    return attended, grad_q, grad_k, grad_v, grad_state, grad_gain.reshape(width)


def solution(mesh):
    tokens = P("seq", "head")
    specs = (P("head", None, None), P("head"))
    return jax.shard_map(
        on_device,
        mesh=mesh,
        in_specs=(tokens,) * 4 + specs,
        out_specs=(tokens,) * 4 + specs,
        check_vma=False,
    )
```

```python
import functools

import jax
import jax.numpy as jnp
from jax import lax
from jax.experimental import pallas as pl
from jax.experimental.pallas import tpu as pltpu
from jax.sharding import PartitionSpec as P

EPS = 1e-05
F32 = jnp.float32
BF16 = jnp.bfloat16
VMEM = 16 * 2**20
PLANE = 4
EXTRA = 16
WHOLE = pl.BlockSpec(memory_space=pltpu.VMEM)
shape = jax.ShapeDtypeStruct


def dot(a, b, ca, cb):
    return lax.dot_general(a, b, (((ca,), (cb,)), ((), ())), preferred_element_type=F32)


def call(kernel, outs, flops, nbytes, **options):
    return pl.pallas_call(
        kernel,
        out_shape=outs,
        compiler_params=pltpu.CompilerParams(vmem_limit_bytes=VMEM),
        cost_estimate=pl.CostEstimate(flops=flops, bytes_accessed=nbytes, transcendentals=0),
        **options,
    )


def cols(h, dim):
    return slice(h * dim, (h + 1) * dim)


def causal(length):
    rows = lax.broadcasted_iota(jnp.int32, (length, length), 0)
    return rows >= lax.broadcasted_iota(jnp.int32, (length, length), 1)


def state_kernel(halves, dim, k_hbm, v_hbm, *refs):
    wide, narrow = refs[: len(halves)], refs[len(halves) : 2 * len(halves)]
    k_ref, v_ref, k_sem, v_sem = refs[2 * len(halves) :]
    k_copy = pltpu.make_async_copy(k_hbm, k_ref, k_sem)
    v_copy = pltpu.make_async_copy(v_hbm, v_ref, v_sem)
    k_copy.start()
    v_copy.start()
    k_copy.wait()
    v_copy.wait()
    for heads, wide_ref, narrow_ref in zip(halves, wide, narrow):
        for i, h in enumerate(heads):
            state = dot(k_ref[:, cols(h, dim)], v_ref[:, cols(h, dim)], 0, 0)
            wide_ref[cols(i, dim), :] = state
            narrow_ref[cols(i, dim), :] = state.astype(BF16)


def scores_kernel(heads, dim, q_ref, k_ref, v_ref, local_ref):
    mask = causal(q_ref.shape[0])
    for h in range(heads):
        c = cols(h, dim)
        scores = jnp.where(mask, dot(q_ref[:, c], k_ref[:, c], 1, 1), 0.0).astype(BF16)
        local_ref[:, c] = dot(scores, v_ref[:, c], 1, 0)


def gathered(partners, parts, rows, reverse):
    mine = lax.axis_index("seq")
    total = None
    for partner, part in zip(partners, parts):
        top = 1 << (partner.bit_length() - 1)
        reached = (mine & top) == (0 if reverse else top)
        term = jnp.where(reached, part[rows, :].astype(F32), 0.0)
        total = term if total is None else total + term
    return total


def unnormed_kernel(heads, dim, partners, first, *refs):
    parts = refs[: len(partners)]
    refs = refs[len(partners) :]
    if not first:
        before, refs = refs[0], refs[1:]
    q_ref, local_ref, cot_ref, carried_ref, gain_ref, un_ref, prefix_ref, sums_ref = refs
    square = product = 0.0
    for i, h in enumerate(heads):
        c, r = cols(h, dim), cols(i, dim)
        prefix = carried_ref[h]
        if parts:
            prefix = prefix + gathered(partners, parts, r, False)
        prefix = prefix.astype(BF16)
        prefix_ref[r, :] = prefix
        un = local_ref[:, c] + dot(q_ref[:, c], prefix, 1, 0)
        un_ref[:, r] = un
        square = square + un * un
        product = product + cot_ref[:, c].astype(F32) * gain_ref[:, c] * un
    square = jnp.sum(square, axis=1, keepdims=True)
    product = jnp.sum(product, axis=1, keepdims=True)
    lane = lax.broadcasted_iota(jnp.int32, sums_ref.shape, 1)
    sums = jnp.where(lane < sums_ref.shape[1] // 2, square, product)
    sums_ref[...] = sums if first else sums + before[...]


def scales(sums_ref, other_ref, width):
    sums = sums_ref[...] + other_ref[...]
    half = sums.shape[1] // 2
    inverse = 1.0 / jnp.sqrt(sums[:, 0:1] / width + EPS)
    return inverse, (sums[:, half : half + 1] * inverse) / width * inverse * inverse


def norm_kernel(heads, dim, width, sums_ref, other_ref, un_ref, cot_ref, gain_ref, q_ref, gun_ref, msg_ref):
    inverse, factor = scales(sums_ref, other_ref, width)
    for i, h in enumerate(heads):
        c, r = cols(h, dim), cols(i, dim)
        un = un_ref[:, r]
        cot = cot_ref[:, c].astype(F32)
        gun = (cot * gain_ref[:, c] * inverse - un * factor).astype(BF16)
        gun_ref[:, r] = gun
        msg_ref[r, :] = dot(q_ref[:, c], gun, 0, 0).astype(BF16)
        row = len(heads) * dim + i
        msg_ref[row : row + 1, :] = jnp.sum(cot * (un * inverse), axis=0, keepdims=True).astype(BF16)
    rest = len(heads) * (dim + 1)
    msg_ref[rest:, :] = jnp.zeros((msg_ref.shape[0] - rest, dim), BF16)


def attended_kernel(halves, dim, width, *refs):
    n = len(halves)
    uns, guns, prefixes = refs[:n], refs[n : 2 * n], refs[2 * n : 3 * n]
    sums_ref, other_ref, gain_ref, k_ref, v_ref, att_ref, gq_ref = refs[3 * n :]
    inverse, _ = scales(sums_ref, other_ref, width)
    mask = causal(k_ref.shape[0])
    for heads, un_ref, gun_ref, prefix_ref in zip(halves, uns, guns, prefixes):
        for i, h in enumerate(heads):
            c, r = cols(h, dim), cols(i, dim)
            att_ref[:, c] = (gain_ref[:, c] * (un_ref[:, r] * inverse)).astype(BF16)
            gun = gun_ref[:, r]
            mixed = jnp.where(mask, dot(gun, v_ref[:, c], 1, 1), 0.0).astype(BF16)
            gq = dot(mixed, k_ref[:, c], 1, 0) + dot(gun, prefix_ref[r, :], 1, 1)
            gq_ref[:, c] = gq.astype(BF16)


def local_kernel(halves, dim, *refs):
    n = len(halves)
    guns = refs[:n]
    q_ref, k_ref, v_ref, gk_ref, gv_ref = refs[n:]
    mask = causal(q_ref.shape[0])
    for heads, gun_ref in zip(halves, guns):
        for i, h in enumerate(heads):
            c = cols(h, dim)
            q, k, gun = q_ref[:, c], k_ref[:, c], gun_ref[:, cols(i, dim)]
            mixed = jnp.where(mask, dot(gun, v_ref[:, c], 1, 1), 0.0).astype(BF16)
            scores = jnp.where(mask, dot(q, k, 1, 1), 0.0).astype(BF16)
            gk_ref[:, c] = dot(mixed, q, 0, 0)
            gv_ref[:, c] = dot(scores, gun, 0, 0)


def final_kernel(heads, dim, partners, first, *refs):
    parts = refs[: len(partners)]
    refs = refs[len(partners) :]
    message_ref, k_ref, v_ref, gk_ref, gv_ref = refs[:5]
    gk_out, gv_out, state_out, gain_out = refs[5 if first else 9 :]
    for i, h in enumerate(heads):
        c, r = cols(h, dim), cols(i, dim)
        total = message_ref[r, :].astype(F32)
        gk, gv = gk_ref[:, c], gv_ref[:, c]
        row = slice(len(heads) * dim + i, len(heads) * dim + i + 1)
        gain = message_ref[row, :].astype(F32)
        if parts:
            suffix = gathered(partners, parts, r, True).astype(BF16)
            gk = gk + dot(v_ref[:, c], suffix, 1, 1)
            gv = gv + dot(k_ref[:, c], suffix, 1, 0)
            total = total + parts[-1][r, :].astype(F32)
            gain = gain + parts[-1][row, :].astype(F32)
        gk_out[:, r] = gk.astype(BF16)
        gv_out[:, r] = gv.astype(BF16)
        state_out[i] = total
        gain_out[:, r] = gain


def swap(message, count, partner):
    return lax.ppermute(message, "seq", [(i, i ^ partner) for i in range(count)])


def scan(messages, owns, count):
    partners, received = [], [[] for _ in messages]
    distance = 1
    if count >= PLANE:
        partners = list(range(1, PLANE))
        for parts, message in zip(received, messages):
            parts.extend(swap(message, count, partner) for partner in partners)
        distance = PLANE
    while distance < count:
        for n, parts in enumerate(received):
            if parts:
                own = messages[n].astype(F32) if owns is None else owns[n]
                got = [part.astype(F32) for part in parts]
                if distance == PLANE:
                    own = (own + got[0]) + (got[1] + got[2])
                else:
                    own = own + got[-1]
                messages[n] = own.astype(BF16)
                if owns is not None:
                    owns[n] = own
        for n, parts in enumerate(received):
            parts.append(swap(messages[n], count, distance))
        partners.append(distance)
        distance *= 2
    return partners, messages, received


def on_device(queries, key_rows, values, cotangent, carried_state, norm_gain):
    length, width = queries.shape
    heads, dim = carried_state.shape[:2]
    count = lax.axis_size("seq")
    head_count = lax.axis_size("head")
    assert count & (count - 1) == 0 and count >= 2 * PLANE
    assert width == heads * dim and heads % 2 == 0
    total_width = width * head_count
    per = heads // 2
    assert per <= EXTRA
    halves = [list(range(per)), list(range(per, heads))]
    gain = norm_gain.reshape(1, width)
    half_f32 = shape((length, per * dim), F32)
    half_bf = shape((length, per * dim), BF16)
    state_f32 = shape((per * dim, dim), F32)
    state_bf = shape((per * dim, dim), BF16)
    tokens_bf = shape((length, width), BF16)
    tokens_f32 = shape((length, width), F32)
    block = 2 * length * dim * dim * heads
    square = 2 * length * length * dim * heads
    size = length * width * 2
    state_size = heads * dim * dim * 2

    hbm = pl.BlockSpec(memory_space=pltpu.HBM)
    states = call(
        functools.partial(state_kernel, halves, dim),
        [state_f32] * 2 + [state_bf] * 2, block, 2 * size + state_size,
        in_specs=[hbm, hbm],
        scratch_shapes=[pltpu.VMEM((length, width), BF16)] * 2 + [pltpu.SemaphoreType.DMA] * 2,
    )(key_rows, values)
    partners, _, received = scan(list(states[2:]), list(states[:2]), count)
    local = call(
        functools.partial(scores_kernel, heads, dim), tokens_f32, 2 * square, 5 * size,
    )(queries, key_rows, values)
    unnormed, prefixes, sums = [], [], ()
    for n, members in enumerate(halves):
        un, prefix, both = call(
            functools.partial(unnormed_kernel, members, dim, partners, n == 0),
            (half_f32, state_bf, shape((length, 128), F32)), block // 2, 3 * size + 4 * state_size,
        )(*received[n], *sums, queries, local, cotangent, carried_state, gain)
        unnormed.append(un)
        prefixes.append(prefix)
        sums = (both,)
    sums = sums[0]
    other = partner = sums
    for step in range(1, head_count):
        partner = lax.ppermute(partner, "head", [(i, (i + 1) % head_count) for i in range(head_count)])
        other = other + partner if step > 1 else partner

    guns, messages = [], []
    for n, members in enumerate(halves):
        gun, message = call(
            functools.partial(norm_kernel, members, dim, total_width),
            (half_bf, shape((per * dim + EXTRA, dim), BF16)), block // 2, 3 * size,
        )(sums, other, unnormed[n], cotangent, gain, queries)
        guns.append(gun)
        messages.append(message)
    partners, messages, received = scan(messages, None, count)
    attended, grad_q = call(
        functools.partial(attended_kernel, halves, dim, total_width),
        (tokens_bf, tokens_bf), 2 * square + block, 8 * size,
    )(*unnormed, *guns, *prefixes, sums, other, gain, key_rows, values)
    local_k, local_v = call(
        functools.partial(local_kernel, halves, dim), (tokens_f32, tokens_f32), 4 * square, 8 * size,
    )(*guns, queries, key_rows, values)

    outs = ()
    for n, members in enumerate(halves):
        operands = (*received[n], messages[n], key_rows, values, local_k, local_v)
        column = functools.partial(lambda at, i: (0, at), n)
        outs = call(
            functools.partial(final_kernel, members, dim, partners, n == 0),
            (tokens_bf, tokens_bf, shape((heads, dim, dim), F32), shape((1, width), F32)),
            block, 5 * size + 4 * state_size,
            grid=(1,),
            in_specs=[WHOLE] * len(operands) + [hbm] * len(outs),
            out_specs=[
                pl.BlockSpec((length, per * dim), column),
                pl.BlockSpec((length, per * dim), column),
                pl.BlockSpec((per, dim, dim), functools.partial(lambda at, i: (at, 0, 0), n)),
                pl.BlockSpec((1, per * dim), column),
            ],
            input_output_aliases={len(operands) + i: i for i in range(len(outs))},
        )(*operands, *outs)
    grad_k, grad_v, grad_state, grad_gain = outs
    return attended, grad_q, grad_k, grad_v, grad_state, grad_gain.reshape(width)


def solution(mesh):
    tokens = P("seq", "head")
    specs = (P("head", None, None), P("head"))
    return jax.shard_map(
        on_device,
        mesh=mesh,
        in_specs=(tokens,) * 4 + specs,
        out_specs=(tokens,) * 4 + specs,
        check_vma=False,
    )
```

```python
import functools

import jax
import jax.numpy as jnp
from jax import lax
from jax.experimental import pallas as pl
from jax.experimental.pallas import tpu as pltpu
from jax.sharding import PartitionSpec as P

EPS = 1e-05
F32 = jnp.float32
BF16 = jnp.bfloat16
VMEM = 16 * 2**20
PLANE = 4
EXTRA = 16
WHOLE = pl.BlockSpec(memory_space=pltpu.VMEM)
shape = jax.ShapeDtypeStruct


def dot(a, b, ca, cb):
    return lax.dot_general(a, b, (((ca,), (cb,)), ((), ())), preferred_element_type=F32)


def call(kernel, outs, flops, nbytes, **options):
    return pl.pallas_call(
        kernel,
        out_shape=outs,
        compiler_params=pltpu.CompilerParams(vmem_limit_bytes=VMEM),
        cost_estimate=pl.CostEstimate(flops=flops, bytes_accessed=nbytes, transcendentals=0),
        **options,
    )


def cols(h, dim):
    return slice(h * dim, (h + 1) * dim)


def causal(length):
    rows = lax.broadcasted_iota(jnp.int32, (length, length), 0)
    return rows >= lax.broadcasted_iota(jnp.int32, (length, length), 1)


def state_kernel(halves, dim, kv_ref, *refs):
    length = kv_ref.shape[0] // 2
    for heads, wide_ref, narrow_ref in zip(halves, refs, refs[len(halves) :]):
        for i, h in enumerate(heads):
            c, r = cols(h, dim), cols(i, dim)
            state = dot(kv_ref[:length, c], kv_ref[length:, c], 0, 0)
            wide_ref[r, :] = state
            narrow_ref[r, :] = state.astype(BF16)


def scores_kernel(heads, dim, q_ref, kv_ref, local_ref):
    length = q_ref.shape[0]
    mask = causal(length)
    for h in range(heads):
        c = cols(h, dim)
        scores = jnp.where(mask, dot(q_ref[:, c], kv_ref[:length, c], 1, 1), 0.0).astype(BF16)
        local_ref[:, c] = dot(scores, kv_ref[length:, c], 1, 0)


def gathered(partners, parts, rows, reverse):
    mine = lax.axis_index("seq")
    total = None
    for partner, part in zip(partners, parts):
        top = 1 << (partner.bit_length() - 1)
        reached = (mine & top) == (0 if reverse else top)
        term = jnp.where(reached, part[rows, :].astype(F32), 0.0)
        total = term if total is None else total + term
    return total


def unnormed_kernel(heads, dim, partners, first, *refs):
    parts = refs[: len(partners)]
    refs = refs[len(partners) :]
    if not first:
        before, refs = refs[0], refs[1:]
    q_ref, local_ref, cot_ref, carried_ref, gain_ref, un_ref, prefix_ref, sums_ref = refs
    square = product = 0.0
    for i, h in enumerate(heads):
        c, r = cols(h, dim), cols(i, dim)
        prefix = carried_ref[h]
        if parts:
            prefix = prefix + gathered(partners, parts, r, False)
        prefix = prefix.astype(BF16)
        prefix_ref[r, :] = prefix
        un = local_ref[:, c] + dot(q_ref[:, c], prefix, 1, 0)
        un_ref[:, r] = un
        square = square + un * un
        product = product + cot_ref[:, c].astype(F32) * gain_ref[:, c] * un
    square = jnp.sum(square, axis=1, keepdims=True)
    product = jnp.sum(product, axis=1, keepdims=True)
    lane = lax.broadcasted_iota(jnp.int32, sums_ref.shape, 1)
    sums = jnp.where(lane < sums_ref.shape[1] // 2, square, product)
    sums_ref[...] = sums if first else sums + before[...]


def scales(sums_ref, other_ref, width):
    sums = sums_ref[...] + other_ref[...]
    half = sums.shape[1] // 2
    inverse = 1.0 / jnp.sqrt(sums[:, 0:1] / width + EPS)
    return inverse, (sums[:, half : half + 1] * inverse) / width * inverse * inverse


def norm_kernel(heads, dim, width, sums_ref, other_ref, un_ref, cot_ref, gain_ref, q_ref, gun_ref, msg_ref):
    inverse, factor = scales(sums_ref, other_ref, width)
    for i, h in enumerate(heads):
        c, r = cols(h, dim), cols(i, dim)
        un = un_ref[:, r]
        cot = cot_ref[:, c].astype(F32)
        gun = (cot * gain_ref[:, c] * inverse - un * factor).astype(BF16)
        gun_ref[:, r] = gun
        msg_ref[r, :] = dot(q_ref[:, c], gun, 0, 0).astype(BF16)
        row = len(heads) * dim + i
        msg_ref[row : row + 1, :] = jnp.sum(cot * (un * inverse), axis=0, keepdims=True).astype(BF16)
    rest = len(heads) * (dim + 1)
    msg_ref[rest:, :] = jnp.zeros((msg_ref.shape[0] - rest, dim), BF16)


def attended_kernel(halves, dim, width, *refs):
    n = len(halves)
    uns, guns, prefixes = refs[:n], refs[n : 2 * n], refs[2 * n : 3 * n]
    sums_ref, other_ref, gain_ref, kv_ref, att_ref, gq_ref = refs[3 * n :]
    inverse, _ = scales(sums_ref, other_ref, width)
    length = kv_ref.shape[0] // 2
    mask = causal(length)
    for heads, un_ref, gun_ref, prefix_ref in zip(halves, uns, guns, prefixes):
        for i, h in enumerate(heads):
            c, r = cols(h, dim), cols(i, dim)
            att_ref[:, c] = (gain_ref[:, c] * (un_ref[:, r] * inverse)).astype(BF16)
            gun = gun_ref[:, r]
            mixed = jnp.where(mask, dot(gun, kv_ref[length:, c], 1, 1), 0.0).astype(BF16)
            gq = dot(mixed, kv_ref[:length, c], 1, 0) + dot(gun, prefix_ref[r, :], 1, 1)
            gq_ref[:, c] = gq.astype(BF16)


def local_kernel(halves, dim, *refs):
    n = len(halves)
    guns = refs[:n]
    q_ref, kv_ref, gk_ref, gv_ref = refs[n:]
    length = q_ref.shape[0]
    mask = causal(length)
    for heads, gun_ref in zip(halves, guns):
        for i, h in enumerate(heads):
            c = cols(h, dim)
            q, k, gun = q_ref[:, c], kv_ref[:length, c], gun_ref[:, cols(i, dim)]
            mixed = jnp.where(mask, dot(gun, kv_ref[length:, c], 1, 1), 0.0).astype(BF16)
            scores = jnp.where(mask, dot(q, k, 1, 1), 0.0).astype(BF16)
            gk_ref[:, c] = dot(mixed, q, 0, 0)
            gv_ref[:, c] = dot(scores, gun, 0, 0)


def final_kernel(heads, dim, partners, first, *refs):
    parts = refs[: len(partners)]
    refs = refs[len(partners) :]
    message_ref, kv_ref, gk_ref, gv_ref = refs[:4]
    gk_out, gv_out, state_out, gain_out = refs[4 if first else 8 :]
    length = kv_ref.shape[0] // 2
    for i, h in enumerate(heads):
        c, r = cols(h, dim), cols(i, dim)
        total = message_ref[r, :].astype(F32)
        gk, gv = gk_ref[:, c], gv_ref[:, c]
        row = slice(len(heads) * dim + i, len(heads) * dim + i + 1)
        gain = message_ref[row, :].astype(F32)
        if parts:
            suffix = gathered(partners, parts, r, True).astype(BF16)
            gk = gk + dot(kv_ref[length:, c], suffix, 1, 1)
            gv = gv + dot(kv_ref[:length, c], suffix, 1, 0)
            total = total + parts[-1][r, :].astype(F32)
            gain = gain + parts[-1][row, :].astype(F32)
        gk_out[:, r] = gk.astype(BF16)
        gv_out[:, r] = gv.astype(BF16)
        state_out[i] = total
        gain_out[:, r] = gain


def swap(message, count, partner):
    return lax.ppermute(message, "seq", [(i, i ^ partner) for i in range(count)])


def scan(messages, owns, count, beside):
    beside = dict(beside)
    received = [[swap(m, count, partner) for partner in range(1, PLANE)] for m in messages]
    partners = list(range(1, PLANE))
    distance = PLANE
    while distance < count:
        for n, parts in enumerate(received):
            got = parts if distance == PLANE else parts[-1:]
            if (n, distance) in beside:
                earlier = received[0]
                earlier[0], operands = lax.optimization_barrier((earlier[0], beside[n, distance][1:]))
                work = beside[n, distance][0](*operands)
                got, beside[n, distance] = lax.optimization_barrier((got, work))
                parts[-len(got) :] = got
            own = messages[n].astype(F32) if owns is None else owns[n]
            got = [part.astype(F32) for part in got]
            own = (own + got[0]) + (got[1] + got[2]) if distance == PLANE else own + got[0]
            messages[n] = own.astype(BF16)
            if owns is not None:
                owns[n] = own
        for n, parts in enumerate(received):
            parts.append(swap(messages[n], count, distance))
        partners.append(distance)
        distance *= 2
    return partners, messages, received, beside


def on_device(queries, key_rows, values, cotangent, carried_state, norm_gain):
    length, width = queries.shape
    heads, dim = carried_state.shape[:2]
    count = lax.axis_size("seq")
    head_count = lax.axis_size("head")
    assert count & (count - 1) == 0 and count > 2 * PLANE
    assert width == heads * dim and heads % 2 == 0
    total_width = width * head_count
    per = heads // 2
    assert per <= EXTRA
    halves = [list(range(per)), list(range(per, heads))]
    gain = norm_gain.reshape(1, width)
    half_f32 = shape((length, per * dim), F32)
    half_bf = shape((length, per * dim), BF16)
    state_f32 = shape((per * dim, dim), F32)
    state_bf = shape((per * dim, dim), BF16)
    tokens_bf = shape((length, width), BF16)
    tokens_f32 = shape((length, width), F32)
    block = 2 * length * dim * dim * heads
    square = 2 * length * length * dim * heads
    size = length * width * 2
    state_size = heads * dim * dim * 2

    kv = jnp.concatenate([key_rows, values], axis=0)
    states = call(
        functools.partial(state_kernel, halves, dim),
        [state_f32] * 2 + [state_bf] * 2, block, 2 * size + state_size,
    )(kv)
    local = (call(
        functools.partial(scores_kernel, heads, dim), tokens_f32, 2 * square, 5 * size,
    ), queries, kv)
    spot = (1, PLANE)
    partners, _, received, done = scan(list(states[2:]), list(states[:2]), count, {spot: local})
    local = done[spot]
    unnormed, prefixes, sums = [], [], ()
    for n, members in enumerate(halves):
        un, prefix, both = call(
            functools.partial(unnormed_kernel, members, dim, partners, n == 0),
            (half_f32, state_bf, shape((length, 128), F32)), block // 2, 3 * size + 4 * state_size,
        )(*received[n], *sums, queries, local, cotangent, carried_state, gain)
        unnormed.append(un)
        prefixes.append(prefix)
        sums = (both,)
    sums = sums[0]
    other = partner = sums
    for step in range(1, head_count):
        partner = lax.ppermute(partner, "head", [(i, (i + 1) % head_count) for i in range(head_count)])
        other = other + partner if step > 1 else partner

    guns, messages = [], []
    for n, members in enumerate(halves):
        gun, message = call(
            functools.partial(norm_kernel, members, dim, total_width),
            (half_bf, shape((per * dim + EXTRA, dim), BF16)), block // 2, 3 * size,
        )(sums, other, unnormed[n], cotangent, gain, queries)
        guns.append(gun)
        messages.append(message)
    outer = (call(
        functools.partial(attended_kernel, halves, dim, total_width),
        (tokens_bf, tokens_bf), 2 * square + block, 8 * size,
    ), *unnormed, *guns, *prefixes, sums, other, gain, kv)
    local_k, local_v = call(
        functools.partial(local_kernel, halves, dim), (tokens_f32, tokens_f32), 4 * square, 8 * size,
    )(*guns, queries, kv)
    partners, messages, received, done = scan(messages, None, count, {spot: outer})
    attended, grad_q = done[spot]

    outs = ()
    for n, members in enumerate(halves):
        operands = (*received[n], messages[n], kv, local_k, local_v)
        column = functools.partial(lambda at, i: (0, at), n)
        outs = call(
            functools.partial(final_kernel, members, dim, partners, n == 0),
            (tokens_bf, tokens_bf, shape((heads, dim, dim), F32), shape((1, width), F32)),
            block, 5 * size + 4 * state_size,
            grid=(1,),
            in_specs=[WHOLE] * len(operands) + [pl.BlockSpec(memory_space=pl.ANY)] * len(outs),
            out_specs=[
                pl.BlockSpec((length, per * dim), column),
                pl.BlockSpec((length, per * dim), column),
                pl.BlockSpec((per, dim, dim), functools.partial(lambda at, i: (at, 0, 0), n)),
                pl.BlockSpec((1, per * dim), column),
            ],
            input_output_aliases={len(operands) + i: i for i in range(len(outs))},
        )(*operands, *outs)
    grad_k, grad_v, grad_state, grad_gain = outs
    return attended, grad_q, grad_k, grad_v, grad_state, grad_gain.reshape(width)


def solution(mesh):
    tokens = P("seq", "head")
    specs = (P("head", None, None), P("head"))
    return jax.shard_map(
        on_device,
        mesh=mesh,
        in_specs=(tokens,) * 4 + specs,
        out_specs=(tokens,) * 4 + specs,
        check_vma=False,
    )
```

```python
import functools

import jax
import jax.numpy as jnp
from jax import lax
from jax.experimental import pallas as pl
from jax.experimental.pallas import tpu as pltpu
from jax.sharding import PartitionSpec as P

EPS = 1e-05
F32 = jnp.float32
BF16 = jnp.bfloat16
VMEM = 16 * 2**20
PLANE = 4
EXTRA = 16
ROWS = 8
WHOLE = pl.BlockSpec(memory_space=pltpu.VMEM)
shape = jax.ShapeDtypeStruct


def dot(a, b, ca, cb):
    return lax.dot_general(a, b, (((ca,), (cb,)), ((), ())), preferred_element_type=F32)


def call(kernel, outs, flops, nbytes, **options):
    return pl.pallas_call(
        kernel,
        out_shape=outs,
        compiler_params=pltpu.CompilerParams(vmem_limit_bytes=VMEM),
        cost_estimate=pl.CostEstimate(flops=flops, bytes_accessed=nbytes, transcendentals=0),
        **options,
    )


def cols(h, dim):
    return slice(h * dim, (h + 1) * dim)


def causal(length, turned=False):
    rows = lax.broadcasted_iota(jnp.int32, (length, length), 1 if turned else 0)
    return rows >= lax.broadcasted_iota(jnp.int32, (length, length), 0 if turned else 1)


def state_kernel(halves, dim, kv_ref, *refs):
    length = kv_ref.shape[0] // 2
    for heads, wide_ref, narrow_ref in zip(halves, refs, refs[len(halves) :]):
        for i, h in enumerate(heads):
            c, r = cols(h, dim), cols(i, dim)
            state = dot(kv_ref[:length, c], kv_ref[length:, c], 0, 0)
            wide_ref[r, :] = state
            narrow_ref[r, :] = state.astype(BF16)


def scores_kernel(heads, dim, q_ref, kv_ref, local_ref, turned_ref):
    length = q_ref.shape[0]
    mask = causal(length)
    for h in range(heads):
        c = cols(h, dim)
        q = q_ref[:, c]
        turned_ref[c, :] = q.T
        scores = jnp.where(mask, dot(q, kv_ref[:length, c], 1, 1), 0.0).astype(BF16)
        local_ref[:, c] = dot(scores, kv_ref[length:, c], 1, 0)


def gathered(partners, parts, rows, reverse):
    mine = lax.axis_index("seq")
    total = None
    for partner, part in zip(partners, parts):
        top = 1 << (partner.bit_length() - 1)
        reached = (mine & top) == (0 if reverse else top)
        term = jnp.where(reached, part[rows, :].astype(F32), 0.0)
        total = term if total is None else total + term
    return total


def unnormed_kernel(heads, dim, partners, first, *refs):
    parts = refs[: len(partners)]
    refs = refs[len(partners) :]
    if not first:
        before, refs = refs[0], refs[1:]
    q_ref, local_ref, cot_ref, carried_ref, gain_ref, un_ref, prefix_ref, sums_ref = refs
    square = product = 0.0
    for i, h in enumerate(heads):
        c, r = cols(h, dim), cols(i, dim)
        prefix = carried_ref[h]
        if parts:
            prefix = prefix + gathered(partners, parts, r, False)
        prefix = prefix.astype(BF16)
        prefix_ref[r, :] = prefix
        un = local_ref[:, c] + dot(q_ref[:, c], prefix, 1, 0)
        un_ref[:, r] = un
        square = square + un * un
        product = product + cot_ref[:, c].astype(F32) * gain_ref[:, c] * un
    square = jnp.sum(square.T, axis=0, keepdims=True)
    product = jnp.sum(product.T, axis=0, keepdims=True)
    row = lax.broadcasted_iota(jnp.int32, sums_ref.shape, 0)
    sums = jnp.where(row < ROWS // 2, square, product)
    sums_ref[...] = sums if first else sums + before[...]


def scales(sums_ref, other_ref, width, dim):
    sums = sums_ref[...] + other_ref[...]
    inverse = lax.rsqrt(sums[0:1, :] / width + EPS)
    factor = (sums[ROWS // 2 : ROWS // 2 + 1, :] * inverse) / width * inverse * inverse
    length = sums.shape[1]
    return [jnp.broadcast_to(row, (dim, length)).T for row in (inverse, factor)]


def norm_kernel(heads, dim, width, sums_ref, other_ref, un_ref, cot_ref, gain_ref, q_ref, gun_ref, msg_ref):
    inverse, factor = scales(sums_ref, other_ref, width, dim)
    for i, h in enumerate(heads):
        c, r = cols(h, dim), cols(i, dim)
        un = un_ref[:, r]
        cot = cot_ref[:, c].astype(F32)
        gun = (cot * gain_ref[:, c] * inverse - un * factor).astype(BF16)
        gun_ref[:, r] = gun
        msg_ref[r, :] = dot(q_ref[c, :], gun, 1, 0).astype(BF16)
        row = len(heads) * dim + i
        msg_ref[row : row + 1, :] = jnp.sum(cot * (un * inverse), axis=0, keepdims=True).astype(BF16)
    rest = len(heads) * (dim + 1)
    msg_ref[rest:, :] = jnp.zeros((msg_ref.shape[0] - rest, dim), BF16)


def attended_kernel(halves, dim, width, *refs):
    n = len(halves)
    uns, guns, prefixes = refs[:n], refs[n : 2 * n], refs[2 * n : 3 * n]
    sums_ref, other_ref, gain_ref, kv_ref, att_ref, gq_ref = refs[3 * n :]
    inverse, _ = scales(sums_ref, other_ref, width, dim)
    length = kv_ref.shape[0] // 2
    mask = causal(length)
    for heads, un_ref, gun_ref, prefix_ref in zip(halves, uns, guns, prefixes):
        for i, h in enumerate(heads):
            c, r = cols(h, dim), cols(i, dim)
            att_ref[:, c] = (gain_ref[:, c] * (un_ref[:, r] * inverse)).astype(BF16)
            gun = gun_ref[:, r]
            mixed = jnp.where(mask, dot(gun, kv_ref[length:, c], 1, 1), 0.0).astype(BF16)
            gq = dot(mixed, kv_ref[:length, c], 1, 0) + dot(gun, prefix_ref[r, :], 1, 1)
            gq_ref[:, c] = gq.astype(BF16)


def local_kernel(halves, dim, *refs):
    n = len(halves)
    guns = refs[:n]
    q_ref, kv_ref, gk_ref, gv_ref = refs[n:]
    length = q_ref.shape[0]
    mask = causal(length, True)
    for heads, gun_ref in zip(halves, guns):
        for i, h in enumerate(heads):
            c = cols(h, dim)
            q, k, gun = q_ref[:, c], kv_ref[:length, c], gun_ref[:, cols(i, dim)]
            mixed = jnp.where(mask, dot(kv_ref[length:, c], gun, 1, 1), 0.0).astype(BF16)
            scores = jnp.where(mask, dot(k, q, 1, 1), 0.0).astype(BF16)
            gk_ref[:, c] = dot(mixed, q, 1, 0)
            gv_ref[:, c] = dot(scores, gun, 1, 0)


def final_kernel(heads, dim, partners, first, *refs):
    parts = refs[: len(partners)]
    refs = refs[len(partners) :]
    message_ref, kv_ref, gk_ref, gv_ref = refs[:4]
    gk_out, gv_out, state_out, gain_out = refs[4 if first else 8 :]
    length = kv_ref.shape[0] // 2
    for i, h in enumerate(heads):
        c, r = cols(h, dim), cols(i, dim)
        total = message_ref[r, :].astype(F32)
        gk, gv = gk_ref[:, c], gv_ref[:, c]
        row = slice(len(heads) * dim + i, len(heads) * dim + i + 1)
        gain = message_ref[row, :].astype(F32)
        if parts:
            suffix = gathered(partners, parts, r, True).astype(BF16)
            gk = gk + dot(kv_ref[length:, c], suffix, 1, 1)
            gv = gv + dot(kv_ref[:length, c], suffix, 1, 0)
            total = total + parts[-1][r, :].astype(F32)
            gain = gain + parts[-1][row, :].astype(F32)
        gk_out[:, r] = gk.astype(BF16)
        gv_out[:, r] = gv.astype(BF16)
        state_out[i] = total
        gain_out[:, r] = gain


def swap(message, count, partner):
    return lax.ppermute(message, "seq", [(i, i ^ partner) for i in range(count)])


def scan(messages, owns, count, beside):
    beside = dict(beside)
    received = [[swap(m, count, partner) for partner in range(1, PLANE)] for m in messages]
    partners = list(range(1, PLANE))
    distance = PLANE
    while distance < count:
        for n, parts in enumerate(received):
            got = parts if distance == PLANE else parts[-1:]
            if (n, distance) in beside:
                earlier = received[0]
                earlier[0], operands = lax.optimization_barrier((earlier[0], beside[n, distance][1:]))
                work = beside[n, distance][0](*operands)
                got, beside[n, distance] = lax.optimization_barrier((got, work))
                parts[-len(got) :] = got
            own = messages[n].astype(F32) if owns is None else owns[n]
            got = [part.astype(F32) for part in got]
            own = (own + got[0]) + (got[1] + got[2]) if distance == PLANE else own + got[0]
            messages[n] = own.astype(BF16)
            if owns is not None:
                owns[n] = own
        for n, parts in enumerate(received):
            parts.append(swap(messages[n], count, distance))
        partners.append(distance)
        distance *= 2
    return partners, messages, received, beside


def on_device(queries, key_rows, values, cotangent, carried_state, norm_gain):
    length, width = queries.shape
    heads, dim = carried_state.shape[:2]
    count = lax.axis_size("seq")
    head_count = lax.axis_size("head")
    assert count & (count - 1) == 0 and count > 2 * PLANE
    assert width == heads * dim and heads % 2 == 0
    total_width = width * head_count
    per = heads // 2
    assert per <= EXTRA
    halves = [list(range(per)), list(range(per, heads))]
    gain = norm_gain.reshape(1, width)
    half_f32 = shape((length, per * dim), F32)
    half_bf = shape((length, per * dim), BF16)
    state_f32 = shape((per * dim, dim), F32)
    state_bf = shape((per * dim, dim), BF16)
    tokens_bf = shape((length, width), BF16)
    tokens_f32 = shape((length, width), F32)
    block = 2 * length * dim * dim * heads
    square = 2 * length * length * dim * heads
    size = length * width * 2
    state_size = heads * dim * dim * 2

    kv = jnp.concatenate([key_rows, values], axis=0)
    states = call(
        functools.partial(state_kernel, halves, dim),
        [state_f32] * 2 + [state_bf] * 2, block, 2 * size + state_size,
    )(kv)
    local = (call(
        functools.partial(scores_kernel, heads, dim),
        (tokens_f32, shape((width, length), BF16)), 2 * square, 5 * size,
    ), queries, kv)
    spot = (1, PLANE)
    partners, _, received, done = scan(list(states[2:]), list(states[:2]), count, {})
    local, turned = local[0](*local[1:])
    unnormed, prefixes, sums = [], [], ()
    for n, members in enumerate(halves):
        un, prefix, both = call(
            functools.partial(unnormed_kernel, members, dim, partners, n == 0),
            (half_f32, state_bf, shape((ROWS, length), F32)), block // 2, 3 * size + 4 * state_size,
        )(*received[n], *sums, queries, local, cotangent, carried_state, gain)
        unnormed.append(un)
        prefixes.append(prefix)
        sums = (both,)
    sums = sums[0]
    other = partner = sums
    for step in range(1, head_count):
        partner = lax.ppermute(partner, "head", [(i, (i + 1) % head_count) for i in range(head_count)])
        other = other + partner if step > 1 else partner

    guns, messages = [], []
    for n, members in enumerate(halves):
        gun, message = call(
            functools.partial(norm_kernel, members, dim, total_width),
            (half_bf, shape((per * dim + EXTRA, dim), BF16)), block // 2, 3 * size,
        )(sums, other, unnormed[n], cotangent, gain, turned)
        guns.append(gun)
        messages.append(message)
    inner = (call(
        functools.partial(local_kernel, halves, dim), (tokens_f32, tokens_f32), 4 * square, 8 * size,
    ), *guns, queries, kv)
    attended, grad_q = call(
        functools.partial(attended_kernel, halves, dim, total_width),
        (tokens_bf, tokens_bf), 2 * square + block, 8 * size,
    )(*unnormed, *guns, *prefixes, sums, other, gain, kv)
    partners, messages, received, done = scan(messages, None, count, {spot: inner})
    local_k, local_v = done[spot]

    outs = ()
    for n, members in enumerate(halves):
        operands = (*received[n], messages[n], kv, local_k, local_v)
        column = functools.partial(lambda at, i: (0, at), n)
        outs = call(
            functools.partial(final_kernel, members, dim, partners, n == 0),
            (tokens_bf, tokens_bf, shape((heads, dim, dim), F32), shape((1, width), F32)),
            block, 5 * size + 4 * state_size,
            grid=(1,),
            in_specs=[WHOLE] * len(operands) + [pl.BlockSpec(memory_space=pl.ANY)] * len(outs),
            out_specs=[
                pl.BlockSpec((length, per * dim), column),
                pl.BlockSpec((length, per * dim), column),
                pl.BlockSpec((per, dim, dim), functools.partial(lambda at, i: (at, 0, 0), n)),
                pl.BlockSpec((1, per * dim), column),
            ],
            input_output_aliases={len(operands) + i: i for i in range(len(outs))},
        )(*operands, *outs)
    grad_k, grad_v, grad_state, grad_gain = outs
    return attended, grad_q, grad_k, grad_v, grad_state, grad_gain.reshape(width)


def solution(mesh):
    tokens = P("seq", "head")
    specs = (P("head", None, None), P("head"))
    return jax.shard_map(
        on_device,
        mesh=mesh,
        in_specs=(tokens,) * 4 + specs,
        out_specs=(tokens,) * 4 + specs,
        check_vma=False,
    )
```

```python
import functools

import jax
import jax.numpy as jnp
from jax import lax
from jax.experimental import pallas as pl
from jax.experimental.pallas import tpu as pltpu
from jax.sharding import PartitionSpec as P

EPS = 1e-05
F32 = jnp.float32
BF16 = jnp.bfloat16
VMEM = 16 * 2**20
PLANE = 4
EXTRA = 16
ROWS = 8
WHOLE = pl.BlockSpec(memory_space=pltpu.VMEM)
shape = jax.ShapeDtypeStruct


def dot(a, b, ca, cb):
    return lax.dot_general(a, b, (((ca,), (cb,)), ((), ())), preferred_element_type=F32)


def call(kernel, outs, flops, nbytes, **options):
    return pl.pallas_call(
        kernel,
        out_shape=outs,
        compiler_params=pltpu.CompilerParams(vmem_limit_bytes=VMEM),
        cost_estimate=pl.CostEstimate(flops=flops, bytes_accessed=nbytes, transcendentals=0),
        **options,
    )


def cols(h, dim):
    return slice(h * dim, (h + 1) * dim)


def causal(length, turned=False):
    rows = lax.broadcasted_iota(jnp.int32, (length, length), 1 if turned else 0)
    return rows >= lax.broadcasted_iota(jnp.int32, (length, length), 0 if turned else 1)


def state_kernel(halves, dim, kv_ref, *refs):
    length = kv_ref.shape[0] // 2
    for heads, wide_ref, narrow_ref in zip(halves, refs, refs[len(halves) :]):
        for i, h in enumerate(heads):
            c, r = cols(h, dim), cols(i, dim)
            state = dot(kv_ref[:length, c], kv_ref[length:, c], 0, 0)
            wide_ref[r, :] = state
            narrow_ref[r, :] = state.astype(BF16)


def scores_kernel(heads, dim, q_ref, kv_ref, local_ref, turned_ref):
    length = q_ref.shape[0]
    mask = causal(length)
    for h in range(heads):
        c = cols(h, dim)
        q = q_ref[:, c]
        turned_ref[c, :] = q.T
        scores = jnp.where(mask, dot(q, kv_ref[:length, c], 1, 1), 0.0).astype(BF16)
        local_ref[:, c] = dot(scores, kv_ref[length:, c], 1, 0)


def gathered(partners, parts, rows, reverse):
    mine = lax.axis_index("seq")
    total = None
    for partner, part in zip(partners, parts):
        top = 1 << (partner.bit_length() - 1)
        reached = (mine & top) == (0 if reverse else top)
        term = jnp.where(reached, part[rows, :].astype(F32), 0.0)
        total = term if total is None else total + term
    return total


def unnormed_kernel(heads, dim, partners, first, *refs):
    parts = refs[: len(partners)]
    refs = refs[len(partners) :]
    if not first:
        before, refs = refs[0], refs[1:]
    q_ref, local_ref, cot_ref, carried_ref, gain_ref, un_ref, prefix_ref, sums_ref = refs
    square = product = 0.0
    for i, h in enumerate(heads):
        c, r = cols(h, dim), cols(i, dim)
        prefix = (carried_ref[h] + gathered(partners, parts, r, False)).astype(BF16)
        prefix_ref[r, :] = prefix
        un = local_ref[:, c] + dot(q_ref[:, c], prefix, 1, 0)
        un_ref[:, r] = un
        square = square + un * un
        product = product + cot_ref[:, c].astype(F32) * gain_ref[:, c] * un
    square = jnp.sum(square.T, axis=0, keepdims=True)
    product = jnp.sum(product.T, axis=0, keepdims=True)
    row = lax.broadcasted_iota(jnp.int32, sums_ref.shape, 0)
    sums = jnp.where(row < ROWS // 2, square, product)
    sums_ref[...] = sums if first else sums + before[...]


def scales(sums_ref, other_ref, width, dim):
    sums = sums_ref[...] + other_ref[...]
    inverse = lax.rsqrt(sums[0:1, :] / width + EPS)
    factor = (sums[ROWS // 2 : ROWS // 2 + 1, :] * inverse) / width * inverse * inverse
    length = sums.shape[1]
    return [jnp.broadcast_to(row, (dim, length)).T for row in (inverse, factor)]


def norm_kernel(heads, dim, width, sums_ref, other_ref, un_ref, cot_ref, gain_ref, q_ref, gun_ref, msg_ref):
    inverse, factor = scales(sums_ref, other_ref, width, dim)
    row = lax.broadcasted_iota(jnp.int32, (EXTRA, dim), 0)
    gains = jnp.zeros((EXTRA, dim), F32)
    for i, h in enumerate(heads):
        c, r = cols(h, dim), cols(i, dim)
        un = un_ref[:, r]
        cot = cot_ref[:, c].astype(F32)
        gun = (cot * gain_ref[:, c] * inverse - un * factor).astype(BF16)
        gun_ref[:, r] = gun
        msg_ref[r, :] = dot(q_ref[c, :], gun, 1, 0).astype(BF16)
        gains = jnp.where(row == i, jnp.sum(cot * (un * inverse), axis=0, keepdims=True), gains)
    msg_ref[len(heads) * dim :, :] = gains.astype(BF16)


def attended_kernel(halves, dim, width, *refs):
    n = len(halves)
    uns, guns, prefixes = refs[:n], refs[n : 2 * n], refs[2 * n : 3 * n]
    sums_ref, other_ref, gain_ref, kv_ref, att_ref, gq_ref = refs[3 * n :]
    inverse, _ = scales(sums_ref, other_ref, width, dim)
    length = kv_ref.shape[0] // 2
    mask = causal(length)
    for heads, un_ref, gun_ref, prefix_ref in zip(halves, uns, guns, prefixes):
        for i, h in enumerate(heads):
            c, r = cols(h, dim), cols(i, dim)
            att_ref[:, c] = (gain_ref[:, c] * (un_ref[:, r] * inverse)).astype(BF16)
            gun = gun_ref[:, r]
            mixed = jnp.where(mask, dot(gun, kv_ref[length:, c], 1, 1), 0.0).astype(BF16)
            gq = dot(mixed, kv_ref[:length, c], 1, 0) + dot(gun, prefix_ref[r, :], 1, 1)
            gq_ref[:, c] = gq.astype(BF16)


def local_kernel(halves, dim, *refs):
    n = len(halves)
    guns = refs[:n]
    q_ref, kv_ref, gk_ref, gv_ref = refs[n:]
    length = q_ref.shape[0]
    mask = causal(length, True)
    for heads, gun_ref in zip(halves, guns):
        for i, h in enumerate(heads):
            c = cols(h, dim)
            q, k, gun = q_ref[:, c], kv_ref[:length, c], gun_ref[:, cols(i, dim)]
            mixed = jnp.where(mask, dot(kv_ref[length:, c], gun, 1, 1), 0.0).astype(BF16)
            scores = jnp.where(mask, dot(k, q, 1, 1), 0.0).astype(BF16)
            gk_ref[:, c] = dot(mixed, q, 1, 0)
            gv_ref[:, c] = dot(scores, gun, 1, 0)


def final_kernel(heads, dim, partners, first, *refs):
    parts = refs[: len(partners)]
    refs = refs[len(partners) :]
    message_ref, kv_ref, gk_ref, gv_ref = refs[:4]
    gk_out, gv_out, state_out, gain_out = refs[4 if first else 8 :]
    length = kv_ref.shape[0] // 2
    tail = slice(len(heads) * dim, len(heads) * dim + EXTRA)
    gains = message_ref[tail, :].astype(F32) + parts[-1][tail, :].astype(F32)
    for i, h in enumerate(heads):
        c, r = cols(h, dim), cols(i, dim)
        suffix = gathered(partners, parts, r, True).astype(BF16)
        gk = gk_ref[:, c] + dot(kv_ref[length:, c], suffix, 1, 1)
        gv = gv_ref[:, c] + dot(kv_ref[:length, c], suffix, 1, 0)
        gk_out[:, r] = gk.astype(BF16)
        gv_out[:, r] = gv.astype(BF16)
        state_out[i] = message_ref[r, :].astype(F32) + parts[-1][r, :].astype(F32)
        gain_out[:, r] = gains[i : i + 1, :]


def swap(message, count, partner):
    return lax.ppermute(message, "seq", [(i, i ^ partner) for i in range(count)])


def scan(messages, owns, count, beside):
    beside = dict(beside)
    received = [[swap(m, count, partner) for partner in range(1, PLANE)] for m in messages]
    partners = list(range(1, PLANE))
    distance = PLANE
    while distance < count:
        for n, parts in enumerate(received):
            got = parts if distance == PLANE else parts[-1:]
            if (n, distance) in beside:
                earlier = received[0]
                earlier[0], operands = lax.optimization_barrier((earlier[0], beside[n, distance][1:]))
                work = beside[n, distance][0](*operands)
                got, beside[n, distance] = lax.optimization_barrier((got, work))
                parts[-len(got) :] = got
            own = messages[n].astype(F32) if owns is None else owns[n]
            got = [part.astype(F32) for part in got]
            own = (own + got[0]) + (got[1] + got[2]) if distance == PLANE else own + got[0]
            messages[n] = own.astype(BF16)
            if owns is not None:
                owns[n] = own
        for n, parts in enumerate(received):
            parts.append(swap(messages[n], count, distance))
        partners.append(distance)
        distance *= 2
    return partners, messages, received, beside


def on_device(queries, key_rows, values, cotangent, carried_state, norm_gain):
    length, width = queries.shape
    heads, dim = carried_state.shape[:2]
    count = lax.axis_size("seq")
    head_count = lax.axis_size("head")
    assert count & (count - 1) == 0 and count > 2 * PLANE
    assert width == heads * dim and heads % 2 == 0
    total_width = width * head_count
    per = heads // 2
    assert per <= EXTRA
    halves = [list(range(per)), list(range(per, heads))]
    gain = norm_gain.reshape(1, width)
    half_f32 = shape((length, per * dim), F32)
    half_bf = shape((length, per * dim), BF16)
    state_f32 = shape((per * dim, dim), F32)
    state_bf = shape((per * dim, dim), BF16)
    tokens_bf = shape((length, width), BF16)
    tokens_f32 = shape((length, width), F32)
    block = 2 * length * dim * dim * heads
    square = 2 * length * length * dim * heads
    size = length * width * 2
    state_size = heads * dim * dim * 2

    kv = jnp.concatenate([key_rows, values], axis=0)
    states = call(
        functools.partial(state_kernel, halves, dim),
        [state_f32] * 2 + [state_bf] * 2, block, 2 * size + state_size,
    )(kv)
    local = (call(
        functools.partial(scores_kernel, heads, dim),
        (tokens_f32, shape((width, length), BF16)), 2 * square, 5 * size,
    ), queries, kv)
    spot = (1, PLANE)
    partners, _, received, done = scan(list(states[2:]), list(states[:2]), count, {})
    local, turned = local[0](*local[1:])
    unnormed, prefixes, sums = [], [], ()
    for n, members in enumerate(halves):
        un, prefix, both = call(
            functools.partial(unnormed_kernel, members, dim, partners, n == 0),
            (half_f32, state_bf, shape((ROWS, length), F32)), block // 2, 3 * size + 4 * state_size,
        )(*received[n], *sums, queries, local, cotangent, carried_state, gain)
        unnormed.append(un)
        prefixes.append(prefix)
        sums = (both,)
    sums = sums[0]
    other = partner = sums
    for step in range(1, head_count):
        partner = lax.ppermute(partner, "head", [(i, (i + 1) % head_count) for i in range(head_count)])
        other = other + partner if step > 1 else partner

    guns, messages = [], []
    for n, members in enumerate(halves):
        gun, message = call(
            functools.partial(norm_kernel, members, dim, total_width),
            (half_bf, shape((per * dim + EXTRA, dim), BF16)), block // 2, 3 * size,
        )(sums, other, unnormed[n], cotangent, gain, turned)
        guns.append(gun)
        messages.append(message)
    inner = (call(
        functools.partial(local_kernel, halves, dim), (tokens_f32, tokens_f32), 4 * square, 8 * size,
    ), *guns, queries, kv)
    attended, grad_q = call(
        functools.partial(attended_kernel, halves, dim, total_width),
        (tokens_bf, tokens_bf), 2 * square + block, 8 * size,
    )(*unnormed, *guns, *prefixes, sums, other, gain, kv)
    partners, messages, received, done = scan(messages, None, count, {spot: inner})
    local_k, local_v = done[spot]

    outs = ()
    for n, members in enumerate(halves):
        operands = (*received[n], messages[n], kv, local_k, local_v)
        column = functools.partial(lambda at, i: (0, at), n)
        outs = call(
            functools.partial(final_kernel, members, dim, partners, n == 0),
            (tokens_bf, tokens_bf, shape((heads, dim, dim), F32), shape((1, width), F32)),
            block, 5 * size + 4 * state_size,
            grid=(1,),
            in_specs=[WHOLE] * len(operands) + [pl.BlockSpec(memory_space=pl.ANY)] * len(outs),
            out_specs=[
                pl.BlockSpec((length, per * dim), column),
                pl.BlockSpec((length, per * dim), column),
                pl.BlockSpec((per, dim, dim), functools.partial(lambda at, i: (at, 0, 0), n)),
                pl.BlockSpec((1, per * dim), column),
            ],
            input_output_aliases={len(operands) + i: i for i in range(len(outs))},
        )(*operands, *outs)
    grad_k, grad_v, grad_state, grad_gain = outs
    return attended, grad_q, grad_k, grad_v, grad_state, grad_gain.reshape(width)


def solution(mesh):
    tokens = P("seq", "head")
    specs = (P("head", None, None), P("head"))
    return jax.shard_map(
        on_device,
        mesh=mesh,
        in_specs=(tokens,) * 4 + specs,
        out_specs=(tokens,) * 4 + specs,
        check_vma=False,
    )
```

```python
import functools

import jax
import jax.numpy as jnp
from jax import lax
from jax.experimental import pallas as pl
from jax.experimental.pallas import tpu as pltpu
from jax.sharding import PartitionSpec as P

EPS = 1e-05
F32 = jnp.float32
BF16 = jnp.bfloat16
VMEM = 16 * 2**20
PLANE = 4
EXTRA = 16
ROWS = 8
WHOLE = pl.BlockSpec(memory_space=pltpu.VMEM)
shape = jax.ShapeDtypeStruct


def dot(a, b, ca, cb):
    return lax.dot_general(a, b, (((ca,), (cb,)), ((), ())), preferred_element_type=F32)


def call(kernel, outs, flops, nbytes, **options):
    return pl.pallas_call(
        kernel,
        out_shape=outs,
        compiler_params=pltpu.CompilerParams(vmem_limit_bytes=VMEM),
        cost_estimate=pl.CostEstimate(flops=flops, bytes_accessed=nbytes, transcendentals=0),
        **options,
    )


def cols(h, dim):
    return slice(h * dim, (h + 1) * dim)


def causal(length, turned=False):
    rows = lax.broadcasted_iota(jnp.int32, (length, length), 1 if turned else 0)
    return rows >= lax.broadcasted_iota(jnp.int32, (length, length), 0 if turned else 1)


def state_kernel(halves, dim, kv_ref, *refs):
    length = kv_ref.shape[0] // 2
    for heads, wide_ref, narrow_ref in zip(halves, refs, refs[len(halves) :]):
        for i, h in enumerate(heads):
            c, r = cols(h, dim), cols(i, dim)
            state = dot(kv_ref[:length, c], kv_ref[length:, c], 0, 0)
            wide_ref[r, :] = state
            narrow_ref[r, :] = state.astype(BF16)


def scores_kernel(heads, dim, q_ref, kv_ref, local_ref, turned_ref):
    length = q_ref.shape[0]
    mask = causal(length)
    for h in range(heads):
        c = cols(h, dim)
        q = q_ref[:, c]
        turned_ref[c, :] = q.T
        scores = jnp.where(mask, dot(q, kv_ref[:length, c], 1, 1), 0.0).astype(BF16)
        local_ref[:, c] = dot(scores, kv_ref[length:, c], 1, 0)


def gathered(partners, parts, rows, reverse):
    mine = lax.axis_index("seq")
    total = None
    for partner, part in zip(partners, parts):
        top = 1 << (partner.bit_length() - 1)
        reached = (mine & top) == (0 if reverse else top)
        term = jnp.where(reached, part[rows, :].astype(F32), 0.0)
        total = term if total is None else total + term
    return total


def unnormed_kernel(heads, dim, partners, first, *refs):
    parts = refs[: len(partners)]
    refs = refs[len(partners) :]
    if not first:
        before, refs = refs[0], refs[1:]
    q_ref, local_ref, cot_ref, carried_ref, gain_ref, un_ref, prefix_ref, sums_ref = refs
    square = product = 0.0
    for i, h in enumerate(heads):
        c, r = cols(h, dim), cols(i, dim)
        prefix = (carried_ref[h] + gathered(partners, parts, r, False)).astype(BF16)
        prefix_ref[r, :] = prefix
        un = local_ref[:, c] + dot(q_ref[:, c], prefix, 1, 0)
        un_ref[:, r] = un
        square = square + un * un
        product = product + cot_ref[:, c].astype(F32) * gain_ref[:, c] * un
    square = jnp.sum(square.T, axis=0, keepdims=True)
    product = jnp.sum(product.T, axis=0, keepdims=True)
    row = lax.broadcasted_iota(jnp.int32, sums_ref.shape, 0)
    sums = jnp.where(row < ROWS // 2, square, product)
    sums_ref[...] = sums if first else sums + before[...]


def scales(sums_ref, other_ref, width, dim):
    sums = sums_ref[...] + other_ref[...]
    inverse = lax.rsqrt(sums[0:1, :] / width + EPS)
    factor = (sums[ROWS // 2 : ROWS // 2 + 1, :] * inverse) / width * inverse * inverse
    length = sums.shape[1]
    return [jnp.broadcast_to(row, (dim, length)).T for row in (inverse, factor)]


def norm_kernel(heads, dim, width, first, a_ref, b_ref, un_ref, cot_ref, gain_ref, q_ref, gun_ref, msg_ref, *kept):
    if first:
        inverse, factor = scales(a_ref, b_ref, width, dim)
        kept[0][...] = inverse
        kept[1][...] = factor
    else:
        inverse, factor = a_ref[...], b_ref[...]
    row = lax.broadcasted_iota(jnp.int32, (EXTRA, dim), 0)
    gains = jnp.zeros((EXTRA, dim), F32)
    for i, h in enumerate(heads):
        c, r = cols(h, dim), cols(i, dim)
        un = un_ref[:, r]
        cot = cot_ref[:, c].astype(F32)
        gun = (cot * gain_ref[:, c] * inverse - un * factor).astype(BF16)
        gun_ref[:, r] = gun
        msg_ref[r, :] = dot(q_ref[c, :], gun, 1, 0).astype(BF16)
        gains = jnp.where(row == i, jnp.sum(cot * (un * inverse), axis=0, keepdims=True), gains)
    msg_ref[len(heads) * dim :, :] = gains.astype(BF16)


def attended_kernel(halves, dim, *refs):
    n = len(halves)
    uns, guns, prefixes = refs[:n], refs[n : 2 * n], refs[2 * n : 3 * n]
    inverse_ref, gain_ref, kv_ref, att_ref, gq_ref = refs[3 * n :]
    inverse = inverse_ref[...]
    length = kv_ref.shape[0] // 2
    mask = causal(length)
    for heads, un_ref, gun_ref, prefix_ref in zip(halves, uns, guns, prefixes):
        for i, h in enumerate(heads):
            c, r = cols(h, dim), cols(i, dim)
            att_ref[:, c] = (gain_ref[:, c] * (un_ref[:, r] * inverse)).astype(BF16)
            gun = gun_ref[:, r]
            mixed = jnp.where(mask, dot(gun, kv_ref[length:, c], 1, 1), 0.0).astype(BF16)
            gq = dot(mixed, kv_ref[:length, c], 1, 0) + dot(gun, prefix_ref[r, :], 1, 1)
            gq_ref[:, c] = gq.astype(BF16)


def local_kernel(halves, dim, *refs):
    n = len(halves)
    guns = refs[:n]
    q_ref, kv_ref, gk_ref, gv_ref = refs[n:]
    length = q_ref.shape[0]
    mask = causal(length, True)
    for heads, gun_ref in zip(halves, guns):
        for i, h in enumerate(heads):
            c = cols(h, dim)
            q, k, gun = q_ref[:, c], kv_ref[:length, c], gun_ref[:, cols(i, dim)]
            mixed = jnp.where(mask, dot(kv_ref[length:, c], gun, 1, 1), 0.0).astype(BF16)
            scores = jnp.where(mask, dot(k, q, 1, 1), 0.0).astype(BF16)
            gk_ref[:, c] = dot(mixed, q, 1, 0)
            gv_ref[:, c] = dot(scores, gun, 1, 0)


def final_kernel(heads, dim, partners, first, *refs):
    parts = refs[: len(partners)]
    refs = refs[len(partners) :]
    message_ref, kv_ref, gk_ref, gv_ref = refs[:4]
    gk_out, gv_out, state_out, gain_out = refs[4 if first else 8 :]
    length = kv_ref.shape[0] // 2
    tail = slice(len(heads) * dim, len(heads) * dim + EXTRA)
    gains = message_ref[tail, :].astype(F32) + parts[-1][tail, :].astype(F32)
    for i, h in enumerate(heads):
        c, r = cols(h, dim), cols(i, dim)
        suffix = gathered(partners, parts, r, True).astype(BF16)
        gk = gk_ref[:, c] + dot(kv_ref[length:, c], suffix, 1, 1)
        gv = gv_ref[:, c] + dot(kv_ref[:length, c], suffix, 1, 0)
        gk_out[:, r] = gk.astype(BF16)
        gv_out[:, r] = gv.astype(BF16)
        state_out[i] = message_ref[r, :].astype(F32) + parts[-1][r, :].astype(F32)
        gain_out[:, r] = gains[i : i + 1, :]


def swap(message, count, partner):
    return lax.ppermute(message, "seq", [(i, i ^ partner) for i in range(count)])


def scan(messages, owns, count, beside):
    beside = dict(beside)
    received = [[swap(m, count, partner) for partner in range(1, PLANE)] for m in messages]
    partners = list(range(1, PLANE))
    distance = PLANE
    while distance < count:
        for n, parts in enumerate(received):
            got = parts if distance == PLANE else parts[-1:]
            if (n, distance) in beside:
                earlier = received[0]
                earlier[0], operands = lax.optimization_barrier((earlier[0], beside[n, distance][1:]))
                work = beside[n, distance][0](*operands)
                got, beside[n, distance] = lax.optimization_barrier((got, work))
                parts[-len(got) :] = got
            own = messages[n].astype(F32) if owns is None else owns[n]
            got = [part.astype(F32) for part in got]
            own = (own + got[0]) + (got[1] + got[2]) if distance == PLANE else own + got[0]
            messages[n] = own.astype(BF16)
            if owns is not None:
                owns[n] = own
        for n, parts in enumerate(received):
            parts.append(swap(messages[n], count, distance))
        partners.append(distance)
        distance *= 2
    return partners, messages, received, beside


def on_device(queries, key_rows, values, cotangent, carried_state, norm_gain):
    length, width = queries.shape
    heads, dim = carried_state.shape[:2]
    count = lax.axis_size("seq")
    head_count = lax.axis_size("head")
    assert count & (count - 1) == 0 and count > 2 * PLANE
    assert width == heads * dim and heads % 2 == 0
    total_width = width * head_count
    per = heads // 2
    assert per <= EXTRA
    halves = [list(range(per)), list(range(per, heads))]
    gain = norm_gain.reshape(1, width)
    half_f32 = shape((length, per * dim), F32)
    half_bf = shape((length, per * dim), BF16)
    state_f32 = shape((per * dim, dim), F32)
    state_bf = shape((per * dim, dim), BF16)
    tokens_bf = shape((length, width), BF16)
    tokens_f32 = shape((length, width), F32)
    block = 2 * length * dim * dim * heads
    square = 2 * length * length * dim * heads
    size = length * width * 2
    state_size = heads * dim * dim * 2

    kv = jnp.concatenate([key_rows, values], axis=0)
    states = call(
        functools.partial(state_kernel, halves, dim),
        [state_f32] * 2 + [state_bf] * 2, block, 2 * size + state_size,
    )(kv)
    local = (call(
        functools.partial(scores_kernel, heads, dim),
        (tokens_f32, shape((width, length), BF16)), 2 * square, 5 * size,
    ), queries, kv)
    spot = (1, PLANE)
    partners, _, received, done = scan(list(states[2:]), list(states[:2]), count, {})
    local, turned = local[0](*local[1:])
    unnormed, prefixes, sums = [], [], ()
    for n, members in enumerate(halves):
        un, prefix, both = call(
            functools.partial(unnormed_kernel, members, dim, partners, n == 0),
            (half_f32, state_bf, shape((ROWS, length), F32)), block // 2, 3 * size + 4 * state_size,
        )(*received[n], *sums, queries, local, cotangent, carried_state, gain)
        unnormed.append(un)
        prefixes.append(prefix)
        sums = (both,)
    sums = sums[0]
    other = partner = sums
    for step in range(1, head_count):
        partner = lax.ppermute(partner, "head", [(i, (i + 1) % head_count) for i in range(head_count)])
        other = other + partner if step > 1 else partner

    guns, messages, scale = [], [], [sums, other]
    column = shape((length, dim), F32)
    for n, members in enumerate(halves):
        gun, message, *kept = call(
            functools.partial(norm_kernel, members, dim, total_width, n == 0),
            (half_bf, shape((per * dim + EXTRA, dim), BF16)) + (column,) * (2 if n == 0 else 0),
            block // 2, 3 * size,
        )(*scale, unnormed[n], cotangent, gain, turned)
        scale = kept or scale
        guns.append(gun)
        messages.append(message)
    inner = (call(
        functools.partial(local_kernel, halves, dim), (tokens_f32, tokens_f32), 4 * square, 8 * size,
    ), *guns, queries, kv)
    attended, grad_q = call(
        functools.partial(attended_kernel, halves, dim),
        (tokens_bf, tokens_bf), 2 * square + block, 8 * size,
    )(*unnormed, *guns, *prefixes, scale[0], gain, kv)
    partners, messages, received, done = scan(messages, None, count, {spot: inner})
    local_k, local_v = done[spot]

    outs = ()
    for n, members in enumerate(halves):
        operands = (*received[n], messages[n], kv, local_k, local_v)
        column = functools.partial(lambda at, i: (0, at), n)
        outs = call(
            functools.partial(final_kernel, members, dim, partners, n == 0),
            (tokens_bf, tokens_bf, shape((heads, dim, dim), F32), shape((1, width), F32)),
            block, 5 * size + 4 * state_size,
            grid=(1,),
            in_specs=[WHOLE] * len(operands) + [pl.BlockSpec(memory_space=pl.ANY)] * len(outs),
            out_specs=[
                pl.BlockSpec((length, per * dim), column),
                pl.BlockSpec((length, per * dim), column),
                pl.BlockSpec((per, dim, dim), functools.partial(lambda at, i: (at, 0, 0), n)),
                pl.BlockSpec((1, per * dim), column),
            ],
            input_output_aliases={len(operands) + i: i for i in range(len(outs))},
        )(*operands, *outs)
    grad_k, grad_v, grad_state, grad_gain = outs
    return attended, grad_q, grad_k, grad_v, grad_state, grad_gain.reshape(width)


def solution(mesh):
    tokens = P("seq", "head")
    specs = (P("head", None, None), P("head"))
    return jax.shard_map(
        on_device,
        mesh=mesh,
        in_specs=(tokens,) * 4 + specs,
        out_specs=(tokens,) * 4 + specs,
        check_vma=False,
    )
```

```python
import functools

import jax
import jax.numpy as jnp
from jax import lax
from jax.experimental import pallas as pl
from jax.experimental.pallas import tpu as pltpu
from jax.sharding import PartitionSpec as P

EPS = 1e-05
F32 = jnp.float32
BF16 = jnp.bfloat16
VMEM = 16 * 2**20
PLANE = 4
EXTRA = 16
ROWS = 8
WHOLE = pl.BlockSpec(memory_space=pltpu.VMEM)
shape = jax.ShapeDtypeStruct


def dot(a, b, ca, cb):
    return lax.dot_general(a, b, (((ca,), (cb,)), ((), ())), preferred_element_type=F32)


def call(kernel, outs, flops, nbytes, **options):
    return pl.pallas_call(
        kernel,
        out_shape=outs,
        compiler_params=pltpu.CompilerParams(vmem_limit_bytes=VMEM),
        cost_estimate=pl.CostEstimate(flops=flops, bytes_accessed=nbytes, transcendentals=0),
        **options,
    )


def cols(h, dim):
    return slice(h * dim, (h + 1) * dim)


def causal(length, turned=False):
    rows = lax.broadcasted_iota(jnp.int32, (length, length), 1 if turned else 0)
    return rows >= lax.broadcasted_iota(jnp.int32, (length, length), 0 if turned else 1)


def state_kernel(halves, dim, *refs):
    n = len(halves)
    length = refs[0].shape[0] // 2
    for heads, kv_ref, wide_ref, narrow_ref in zip(halves, refs, refs[n:], refs[2 * n :]):
        for i in range(len(heads)):
            r = cols(i, dim)
            state = dot(kv_ref[:length, r], kv_ref[length:, r], 0, 0)
            wide_ref[r, :] = state
            narrow_ref[r, :] = state.astype(BF16)


def scores_kernel(halves, dim, q_ref, *refs):
    n = len(halves)
    local_ref, turned_ref = refs[n:]
    length = q_ref.shape[0]
    mask = causal(length)
    for heads, kv_ref in zip(halves, refs):
        for i, h in enumerate(heads):
            c, r = cols(h, dim), cols(i, dim)
            q = q_ref[:, c]
            turned_ref[c, :] = q.T
            scores = jnp.where(mask, dot(q, kv_ref[:length, r], 1, 1), 0.0).astype(BF16)
            local_ref[:, c] = dot(scores, kv_ref[length:, r], 1, 0)


def gathered(partners, parts, rows, reverse):
    mine = lax.axis_index("seq")
    total = None
    for partner, part in zip(partners, parts):
        top = 1 << (partner.bit_length() - 1)
        reached = (mine & top) == (0 if reverse else top)
        term = jnp.where(reached, part[rows, :].astype(F32), 0.0)
        total = term if total is None else total + term
    return total


def unnormed_kernel(heads, dim, partners, first, *refs):
    parts = refs[: len(partners)]
    refs = refs[len(partners) :]
    if not first:
        before, refs = refs[0], refs[1:]
    q_ref, local_ref, cot_ref, carried_ref, gain_ref, un_ref, prefix_ref, sums_ref = refs
    square = product = 0.0
    for i, h in enumerate(heads):
        c, r = cols(h, dim), cols(i, dim)
        prefix = (carried_ref[h] + gathered(partners, parts, r, False)).astype(BF16)
        prefix_ref[r, :] = prefix
        un = local_ref[:, c] + dot(q_ref[:, c], prefix, 1, 0)
        un_ref[:, r] = un
        square = square + un * un
        product = product + cot_ref[:, c].astype(F32) * gain_ref[:, c] * un
    square = jnp.sum(square.T, axis=0, keepdims=True)
    product = jnp.sum(product.T, axis=0, keepdims=True)
    row = lax.broadcasted_iota(jnp.int32, sums_ref.shape, 0)
    sums = jnp.where(row < ROWS // 2, square, product)
    sums_ref[...] = sums if first else sums + before[...]


def scales(sums_ref, other_ref, width, dim):
    sums = sums_ref[...] + other_ref[...]
    inverse = lax.rsqrt(sums[0:1, :] / width + EPS)
    factor = (sums[ROWS // 2 : ROWS // 2 + 1, :] * inverse) / width * inverse * inverse
    length = sums.shape[1]
    return [jnp.broadcast_to(row, (dim, length)).T for row in (inverse, factor)]


def norm_kernel(halves, n, dim, width, *refs):
    if n == 0:
        uns, refs = refs[2 : 2 + len(halves)], refs[:2] + refs[2 + len(halves) :]
        inverse, factor = scales(refs[0], refs[1], width, dim)
        refs[-2][...] = inverse
        refs[-1][...] = factor
    else:
        uns, refs = {n: refs[2]}, refs[:2] + refs[3:]
        inverse, factor = refs[0][...], refs[1][...]
    cot_ref, gain_ref, q_ref, gun_ref, msg_ref = refs[2:7]
    for i, h in enumerate(halves[n]):
        c, r = cols(h, dim), cols(i, dim)
        cot = cot_ref[:, c].astype(F32)
        gun = (cot * gain_ref[:, c] * inverse - uns[n][:, r] * factor).astype(BF16)
        gun_ref[:, r] = gun
        msg_ref[r, :] = dot(q_ref[c, :], gun, 1, 0).astype(BF16)
    if n == 0:
        row = lax.broadcasted_iota(jnp.int32, (EXTRA, dim), 0)
        gains = jnp.zeros((EXTRA, dim), F32)
        for heads, un_ref in zip(halves, uns):
            for i, h in enumerate(heads):
                normed = un_ref[:, cols(i, dim)] * inverse
                total = jnp.sum(cot_ref[:, cols(h, dim)].astype(F32) * normed, axis=0, keepdims=True)
                gains = jnp.where(row == h, total, gains)
        msg_ref[len(halves[0]) * dim :, :] = gains.astype(BF16)


def attended_kernel(halves, dim, *refs):
    n = len(halves)
    uns, guns, prefixes = refs[:n], refs[n : 2 * n], refs[2 * n : 3 * n]
    kvs = refs[3 * n : 4 * n]
    inverse_ref, gain_ref, att_ref, gq_ref = refs[4 * n :]
    inverse = inverse_ref[...]
    length = kvs[0].shape[0] // 2
    mask = causal(length)
    for heads, un_ref, gun_ref, prefix_ref, kv_ref in zip(halves, uns, guns, prefixes, kvs):
        for i, h in enumerate(heads):
            c, r = cols(h, dim), cols(i, dim)
            att_ref[:, c] = (gain_ref[:, c] * (un_ref[:, r] * inverse)).astype(BF16)
            gun = gun_ref[:, r]
            mixed = jnp.where(mask, dot(gun, kv_ref[length:, r], 1, 1), 0.0).astype(BF16)
            gq = dot(mixed, kv_ref[:length, r], 1, 0) + dot(gun, prefix_ref[r, :], 1, 1)
            gq_ref[:, c] = gq.astype(BF16)


def local_kernel(halves, dim, *refs):
    n = len(halves)
    guns, kvs = refs[:n], refs[n : 2 * n]
    q_ref, gk_ref, gv_ref = refs[2 * n :]
    length = q_ref.shape[0]
    mask = causal(length, True)
    for heads, gun_ref, kv_ref in zip(halves, guns, kvs):
        for i, h in enumerate(heads):
            c, r = cols(h, dim), cols(i, dim)
            q, k, gun = q_ref[:, c], kv_ref[:length, r], gun_ref[:, r]
            mixed = jnp.where(mask, dot(kv_ref[length:, r], gun, 1, 1), 0.0).astype(BF16)
            scores = jnp.where(mask, dot(k, q, 1, 1), 0.0).astype(BF16)
            gk_ref[:, c] = dot(mixed, q, 1, 0)
            gv_ref[:, c] = dot(scores, gun, 1, 0)


def final_kernel(heads, dim, partners, first, *refs):
    parts = refs[: len(partners)]
    message_ref, kv_ref, gk_ref, gv_ref = refs[len(partners) : len(partners) + 4]
    outs = refs[len(partners) + (4 if first else 7) :]
    gk_out, gv_out, state_out = outs[:3]
    length = kv_ref.shape[0] // 2
    for i, h in enumerate(heads):
        c, r = cols(h, dim), cols(i, dim)
        suffix = gathered(partners, parts, r, True).astype(BF16)
        gk = gk_ref[:, c] + dot(kv_ref[length:, r], suffix, 1, 1)
        gv = gv_ref[:, c] + dot(kv_ref[:length, r], suffix, 1, 0)
        gk_out[:, r] = gk.astype(BF16)
        gv_out[:, r] = gv.astype(BF16)
        state_out[i] = message_ref[r, :].astype(F32) + parts[-1][r, :].astype(F32)
    if first:
        tail = slice(len(heads) * dim, len(heads) * dim + EXTRA)
        gains = message_ref[tail, :].astype(F32) + parts[-1][tail, :].astype(F32)
        for h in range(outs[3].shape[1] // dim):
            outs[3][:, cols(h, dim)] = gains[h : h + 1, :]


def swap(message, count, partner):
    return lax.ppermute(message, "seq", [(i, i ^ partner) for i in range(count)])


def scan(messages, owns, count, beside):
    beside = dict(beside)
    received = [[swap(m, count, partner) for partner in range(1, PLANE)] for m in messages]
    partners = list(range(1, PLANE))
    distance = PLANE
    while distance < count:
        for n, parts in enumerate(received):
            got = parts if distance == PLANE else parts[-1:]
            if (n, distance) in beside:
                earlier = received[0]
                earlier[0], operands = lax.optimization_barrier((earlier[0], beside[n, distance][1:]))
                work = beside[n, distance][0](*operands)
                got, beside[n, distance] = lax.optimization_barrier((got, work))
                parts[-len(got) :] = got
            own = messages[n].astype(F32) if owns is None else owns[n]
            got = [part.astype(F32) for part in got]
            own = (own + got[0]) + (got[1] + got[2]) if distance == PLANE else own + got[0]
            messages[n] = own.astype(BF16)
            if owns is not None:
                owns[n] = own
        for n, parts in enumerate(received):
            parts.append(swap(messages[n], count, distance))
        partners.append(distance)
        distance *= 2
    return partners, messages, received, beside


def on_device(queries, key_rows, values, cotangent, carried_state, norm_gain):
    length, width = queries.shape
    heads, dim = carried_state.shape[:2]
    count = lax.axis_size("seq")
    head_count = lax.axis_size("head")
    assert count & (count - 1) == 0 and count > 2 * PLANE
    assert width == heads * dim and heads % 2 == 0
    total_width = width * head_count
    per = heads // 2
    assert heads <= EXTRA
    halves = [list(range(per)), list(range(per, heads))]
    gain = norm_gain.reshape(1, width)
    half_f32 = shape((length, per * dim), F32)
    half_bf = shape((length, per * dim), BF16)
    state_f32 = shape((per * dim, dim), F32)
    state_bf = shape((per * dim, dim), BF16)
    tokens_bf = shape((length, width), BF16)
    tokens_f32 = shape((length, width), F32)
    block = 2 * length * dim * dim * heads
    square = 2 * length * length * dim * heads
    size = length * width * 2
    state_size = heads * dim * dim * 2

    kvs = [
        jnp.concatenate([part[:, n * per * dim : (n + 1) * per * dim] for part in (key_rows, values)], axis=0)
        for n in range(len(halves))
    ]
    states = call(
        functools.partial(state_kernel, halves, dim),
        [state_f32] * 2 + [state_bf] * 2, block, 2 * size + state_size,
    )(*kvs)
    local = (call(
        functools.partial(scores_kernel, halves, dim),
        (tokens_f32, shape((width, length), BF16)), 2 * square, 5 * size,
    ), queries, *kvs)
    spot = (1, PLANE)
    partners, _, received, done = scan(list(states[2:]), list(states[:2]), count, {})
    local, turned = local[0](*local[1:])
    unnormed, prefixes, sums = [], [], ()
    for n, members in enumerate(halves):
        un, prefix, both = call(
            functools.partial(unnormed_kernel, members, dim, partners, n == 0),
            (half_f32, state_bf, shape((ROWS, length), F32)), block // 2, 3 * size + 4 * state_size,
        )(*received[n], *sums, queries, local, cotangent, carried_state, gain)
        unnormed.append(un)
        prefixes.append(prefix)
        sums = (both,)
    sums = sums[0]
    other = partner = sums
    for step in range(1, head_count):
        partner = lax.ppermute(partner, "head", [(i, (i + 1) % head_count) for i in range(head_count)])
        other = other + partner if step > 1 else partner

    guns, messages, scale = [], [], [sums, other]
    column = shape((length, dim), F32)
    for n, members in enumerate(halves):
        gun, message, *kept = call(
            functools.partial(norm_kernel, halves, n, dim, total_width),
            (half_bf, shape((per * dim + (EXTRA if n == 0 else 0), dim), BF16)) + (column,) * (2 if n == 0 else 0),
            block // 2, 3 * size,
        )(*scale, *(unnormed if n == 0 else unnormed[n:]), cotangent, gain, turned)
        scale = kept or scale
        guns.append(gun)
        messages.append(message)
    inner = (call(
        functools.partial(local_kernel, halves, dim), (tokens_f32, tokens_f32), 4 * square, 8 * size,
    ), *guns, *kvs, queries)
    attended, grad_q = call(
        functools.partial(attended_kernel, halves, dim),
        (tokens_bf, tokens_bf), 2 * square + block, 8 * size,
    )(*unnormed, *guns, *prefixes, *kvs, scale[0], gain)
    partners, messages, received, done = scan(messages, None, count, {spot: inner})
    local_k, local_v = done[spot]

    outs = ()
    for n, members in enumerate(halves):
        operands = (*received[n], messages[n], kvs[n], local_k, local_v)
        column = functools.partial(lambda at, i: (0, at), n)
        results = [tokens_bf, tokens_bf, shape((heads, dim, dim), F32)]
        out_specs = [
            pl.BlockSpec((length, per * dim), column),
            pl.BlockSpec((length, per * dim), column),
            pl.BlockSpec((per, dim, dim), functools.partial(lambda at, i: (at, 0, 0), n)),
        ]
        if n == 0:
            results.append(shape((1, width), F32))
            out_specs.append(pl.BlockSpec((1, width), lambda i: (0, 0)))
        outs = call(
            functools.partial(final_kernel, members, dim, partners, n == 0), results, block, 5 * size + 4 * state_size,
            grid=(1,),
            in_specs=[WHOLE] * len(operands) + [pl.BlockSpec(memory_space=pl.ANY)] * len(outs),
            out_specs=out_specs,
            input_output_aliases={len(operands) + i: i for i in range(len(outs))},
        )(*operands, *outs)
        if n == 0:
            outs, grad_gain = outs[:3], outs[3]
    grad_k, grad_v, grad_state = outs
    return attended, grad_q, grad_k, grad_v, grad_state, grad_gain.reshape(width)


def solution(mesh):
    tokens = P("seq", "head")
    specs = (P("head", None, None), P("head"))
    return jax.shard_map(
        on_device,
        mesh=mesh,
        in_specs=(tokens,) * 4 + specs,
        out_specs=(tokens,) * 4 + specs,
        check_vma=False,
    )
```

```python
import functools

import jax
import jax.numpy as jnp
from jax import lax
from jax.experimental import pallas as pl
from jax.experimental.pallas import tpu as pltpu
from jax.sharding import PartitionSpec as P

EPS = 1e-05
F32 = jnp.float32
BF16 = jnp.bfloat16
VMEM = 16 * 2**20
PLANE = 4
EXTRA = 16
ROWS = 8
WHOLE = pl.BlockSpec(memory_space=pltpu.VMEM)
shape = jax.ShapeDtypeStruct


def dot(a, b, ca, cb):
    return lax.dot_general(a, b, (((ca,), (cb,)), ((), ())), preferred_element_type=F32)


def call(kernel, outs, flops, nbytes, **options):
    return pl.pallas_call(
        kernel,
        out_shape=outs,
        compiler_params=pltpu.CompilerParams(vmem_limit_bytes=VMEM),
        cost_estimate=pl.CostEstimate(flops=flops, bytes_accessed=nbytes, transcendentals=0),
        **options,
    )


def cols(h, dim):
    return slice(h * dim, (h + 1) * dim)


def causal(length, turned=False):
    rows = lax.broadcasted_iota(jnp.int32, (length, length), 1 if turned else 0)
    return rows >= lax.broadcasted_iota(jnp.int32, (length, length), 0 if turned else 1)


def state_kernel(halves, dim, *refs):
    n = len(halves)
    length = refs[0].shape[0] // 2
    for heads, kv_ref, wide_ref, narrow_ref in zip(halves, refs, refs[n:], refs[2 * n :]):
        for i in range(len(heads)):
            r = cols(i, dim)
            state = dot(kv_ref[:length, r], kv_ref[length:, r], 0, 0)
            wide_ref[r, :] = state
            narrow_ref[r, :] = state.astype(BF16)


def scores_kernel(halves, dim, q_ref, *refs):
    n = len(halves)
    local_ref, turned_ref = refs[n:]
    length = q_ref.shape[0]
    mask = causal(length)
    for heads, kv_ref in zip(halves, refs):
        for i, h in enumerate(heads):
            c, r = cols(h, dim), cols(i, dim)
            q = q_ref[:, c]
            turned_ref[c, :] = q.T
            scores = jnp.where(mask, dot(q, kv_ref[:length, r], 1, 1), 0.0).astype(BF16)
            local_ref[:, c] = dot(scores, kv_ref[length:, r], 1, 0)


def gathered(partners, parts, rows, reverse):
    mine = lax.axis_index("seq")
    total = None
    for partner, part in zip(partners, parts):
        top = 1 << (partner.bit_length() - 1)
        reached = (mine & top) == (0 if reverse else top)
        term = jnp.where(reached, part[rows, :].astype(F32), 0.0)
        total = term if total is None else total + term
    return total


def partial_kernel(heads, dim, partners, reverse, *refs):
    parts, out_ref = refs[: len(partners)], refs[-1]
    for i, h in enumerate(heads):
        r = cols(i, dim)
        total = gathered(partners, parts, r, reverse)
        out_ref[r, :] = total if reverse else refs[len(partners)][h] + total


def unnormed_kernel(heads, dim, partners, first, *refs):
    parts = refs[: len(partners)]
    refs = refs[len(partners) :]
    if not first:
        before, refs = refs[0], refs[1:]
    q_ref, local_ref, cot_ref, carried_ref, gain_ref, un_ref, prefix_ref, sums_ref = refs
    square = product = 0.0
    for i, h in enumerate(heads):
        c, r = cols(h, dim), cols(i, dim)
        start = carried_ref[h] if first else carried_ref[r, :]
        prefix = (start + gathered(partners, parts, r, False)).astype(BF16)
        prefix_ref[r, :] = prefix
        un = local_ref[:, c] + dot(q_ref[:, c], prefix, 1, 0)
        un_ref[:, r] = un
        square = square + un * un
        product = product + cot_ref[:, c].astype(F32) * gain_ref[:, c] * un
    square = jnp.sum(square.T, axis=0, keepdims=True)
    product = jnp.sum(product.T, axis=0, keepdims=True)
    row = lax.broadcasted_iota(jnp.int32, sums_ref.shape, 0)
    sums = jnp.where(row < ROWS // 2, square, product)
    sums_ref[...] = sums if first else sums + before[...]


def scales(sums_ref, other_ref, width, dim):
    sums = sums_ref[...] + other_ref[...]
    inverse = lax.rsqrt(sums[0:1, :] / width + EPS)
    factor = (sums[ROWS // 2 : ROWS // 2 + 1, :] * inverse) / width * inverse * inverse
    length = sums.shape[1]
    return [jnp.broadcast_to(row, (dim, length)).T for row in (inverse, factor)]


def norm_kernel(halves, n, dim, width, *refs):
    if n == 0:
        uns, refs = refs[2 : 2 + len(halves)], refs[:2] + refs[2 + len(halves) :]
        inverse, factor = scales(refs[0], refs[1], width, dim)
        refs[-2][...] = inverse
        refs[-1][...] = factor
    else:
        uns, refs = {n: refs[2]}, refs[:2] + refs[3:]
        inverse, factor = refs[0][...], refs[1][...]
    cot_ref, gain_ref, q_ref, gun_ref, msg_ref = refs[2:7]
    for i, h in enumerate(halves[n]):
        c, r = cols(h, dim), cols(i, dim)
        cot = cot_ref[:, c].astype(F32)
        gun = (cot * gain_ref[:, c] * inverse - uns[n][:, r] * factor).astype(BF16)
        gun_ref[:, r] = gun
        msg_ref[r, :] = dot(q_ref[c, :], gun, 1, 0).astype(BF16)
    if n == 0:
        row = lax.broadcasted_iota(jnp.int32, (EXTRA, dim), 0)
        gains = jnp.zeros((EXTRA, dim), F32)
        for heads, un_ref in zip(halves, uns):
            for i, h in enumerate(heads):
                normed = un_ref[:, cols(i, dim)] * inverse
                total = jnp.sum(cot_ref[:, cols(h, dim)].astype(F32) * normed, axis=0, keepdims=True)
                gains = jnp.where(row == h, total, gains)
        msg_ref[len(halves[0]) * dim :, :] = gains.astype(BF16)


def attended_kernel(halves, dim, *refs):
    n = len(halves)
    uns, guns, prefixes = refs[:n], refs[n : 2 * n], refs[2 * n : 3 * n]
    kvs = refs[3 * n : 4 * n]
    inverse_ref, gain_ref, att_ref, gq_ref = refs[4 * n :]
    inverse = inverse_ref[...]
    length = kvs[0].shape[0] // 2
    mask = causal(length)
    for heads, un_ref, gun_ref, prefix_ref, kv_ref in zip(halves, uns, guns, prefixes, kvs):
        for i, h in enumerate(heads):
            c, r = cols(h, dim), cols(i, dim)
            att_ref[:, c] = (gain_ref[:, c] * (un_ref[:, r] * inverse)).astype(BF16)
            gun = gun_ref[:, r]
            mixed = jnp.where(mask, dot(gun, kv_ref[length:, r], 1, 1), 0.0).astype(BF16)
            gq = dot(mixed, kv_ref[:length, r], 1, 0) + dot(gun, prefix_ref[r, :], 1, 1)
            gq_ref[:, c] = gq.astype(BF16)


def local_kernel(halves, dim, *refs):
    n = len(halves)
    guns, kvs = refs[:n], refs[n : 2 * n]
    q_ref, gk_ref, gv_ref = refs[2 * n :]
    length = q_ref.shape[0]
    mask = causal(length, True)
    for heads, gun_ref, kv_ref in zip(halves, guns, kvs):
        for i, h in enumerate(heads):
            c, r = cols(h, dim), cols(i, dim)
            q, k, gun = q_ref[:, c], kv_ref[:length, r], gun_ref[:, r]
            mixed = jnp.where(mask, dot(kv_ref[length:, r], gun, 1, 1), 0.0).astype(BF16)
            scores = jnp.where(mask, dot(k, q, 1, 1), 0.0).astype(BF16)
            gk_ref[:, c] = dot(mixed, q, 1, 0)
            gv_ref[:, c] = dot(scores, gun, 1, 0)


def final_kernel(heads, dim, partners, first, *refs):
    parts = refs[: len(partners)]
    message_ref, kv_ref, gk_ref, gv_ref = refs[len(partners) : len(partners) + 4]
    outs = refs[len(partners) + (4 if first else 8) :]
    gk_out, gv_out, state_out = outs[:3]
    length = kv_ref.shape[0] // 2
    for i, h in enumerate(heads):
        c, r = cols(h, dim), cols(i, dim)
        suffix = gathered(partners, parts, r, True)
        if not first:
            suffix = suffix + refs[len(partners) + 4][r, :]
        suffix = suffix.astype(BF16)
        gk = gk_ref[:, c] + dot(kv_ref[length:, r], suffix, 1, 1)
        gv = gv_ref[:, c] + dot(kv_ref[:length, r], suffix, 1, 0)
        gk_out[:, r] = gk.astype(BF16)
        gv_out[:, r] = gv.astype(BF16)
        state_out[i] = message_ref[r, :].astype(F32) + parts[-1][r, :].astype(F32)
    if first:
        tail = slice(len(heads) * dim, len(heads) * dim + EXTRA)
        gains = message_ref[tail, :].astype(F32) + parts[-1][tail, :].astype(F32)
        for h in range(outs[3].shape[1] // dim):
            outs[3][:, cols(h, dim)] = gains[h : h + 1, :]


def swap(message, count, partner):
    return lax.ppermute(message, "seq", [(i, i ^ partner) for i in range(count)])


def scan(messages, owns, count, beside):
    beside = dict(beside)
    received = [[swap(m, count, partner) for partner in range(1, PLANE)] for m in messages]
    partners = list(range(1, PLANE))
    distance = PLANE
    while distance < count:
        for n, parts in enumerate(received):
            got = parts if distance == PLANE else parts[-1:]
            if (n, distance) in beside:
                earlier = received[0]
                earlier[0], operands = lax.optimization_barrier((earlier[0], beside[n, distance][1:]))
                work = beside[n, distance][0](*operands)
                got, beside[n, distance] = lax.optimization_barrier((got, work))
                parts[-len(got) :] = got
            own = messages[n].astype(F32) if owns is None else owns[n]
            got = [part.astype(F32) for part in got]
            own = (own + got[0]) + (got[1] + got[2]) if distance == PLANE else own + got[0]
            messages[n] = own.astype(BF16)
            if owns is not None:
                owns[n] = own
        for n, parts in enumerate(received):
            parts.append(swap(messages[n], count, distance))
        partners.append(distance)
        distance *= 2
    return partners, messages, received, beside


def on_device(queries, key_rows, values, cotangent, carried_state, norm_gain):
    length, width = queries.shape
    heads, dim = carried_state.shape[:2]
    count = lax.axis_size("seq")
    head_count = lax.axis_size("head")
    assert count & (count - 1) == 0 and count > 2 * PLANE
    assert width == heads * dim and heads % 2 == 0
    total_width = width * head_count
    per = heads // 2
    assert heads <= EXTRA
    halves = [list(range(per)), list(range(per, heads))]
    gain = norm_gain.reshape(1, width)
    half_f32 = shape((length, per * dim), F32)
    half_bf = shape((length, per * dim), BF16)
    state_f32 = shape((per * dim, dim), F32)
    state_bf = shape((per * dim, dim), BF16)
    tokens_bf = shape((length, width), BF16)
    tokens_f32 = shape((length, width), F32)
    block = 2 * length * dim * dim * heads
    square = 2 * length * length * dim * heads
    size = length * width * 2
    state_size = heads * dim * dim * 2

    kvs = [
        jnp.concatenate([part[:, n * per * dim : (n + 1) * per * dim] for part in (key_rows, values)], axis=0)
        for n in range(len(halves))
    ]
    states = call(
        functools.partial(state_kernel, halves, dim),
        [state_f32] * 2 + [state_bf] * 2, block, 2 * size + state_size,
    )(*kvs)
    local = (call(
        functools.partial(scores_kernel, halves, dim),
        (tokens_f32, shape((width, length), BF16)), 2 * square, 5 * size,
    ), queries, *kvs)
    spot = (1, PLANE)
    partners, _, received, done = scan(list(states[2:]), list(states[:2]), count, {})
    local, turned = local[0](*local[1:])
    unnormed, prefixes, sums = [], [], ()
    ahead = functools.partial(partial_kernel, halves[1], dim, partners[:-1])
    start = call(functools.partial(ahead, False), state_f32, 0, 5 * state_size)(*received[1][:-1], carried_state)
    for n, members in enumerate(halves):
        last = slice(0 if n == 0 else -1, None)
        un, prefix, both = call(
            functools.partial(unnormed_kernel, members, dim, partners[last], n == 0),
            (half_f32, state_bf, shape((ROWS, length), F32)), block // 2, 3 * size + 4 * state_size,
        )(*received[n][last], *sums, queries, local, cotangent, carried_state if n == 0 else start, gain)
        unnormed.append(un)
        prefixes.append(prefix)
        sums = (both,)
    sums = sums[0]
    other = partner = sums
    for step in range(1, head_count):
        partner = lax.ppermute(partner, "head", [(i, (i + 1) % head_count) for i in range(head_count)])
        other = other + partner if step > 1 else partner

    guns, messages, scale = [], [], [sums, other]
    column = shape((length, dim), F32)
    for n, members in enumerate(halves):
        gun, message, *kept = call(
            functools.partial(norm_kernel, halves, n, dim, total_width),
            (half_bf, shape((per * dim + (EXTRA if n == 0 else 0), dim), BF16)) + (column,) * (2 if n == 0 else 0),
            block // 2, 3 * size,
        )(*scale, *(unnormed if n == 0 else unnormed[n:]), cotangent, gain, turned)
        scale = kept or scale
        guns.append(gun)
        messages.append(message)
    inner = (call(
        functools.partial(local_kernel, halves, dim), (tokens_f32, tokens_f32), 4 * square, 8 * size,
    ), *guns, *kvs, queries)
    attended, grad_q = call(
        functools.partial(attended_kernel, halves, dim),
        (tokens_bf, tokens_bf), 2 * square + block, 8 * size,
    )(*unnormed, *guns, *prefixes, *kvs, scale[0], gain)
    partners, messages, received, done = scan(messages, None, count, {spot: inner})
    local_k, local_v = done[spot]

    outs = ()
    start = call(functools.partial(ahead, True), state_f32, 0, 5 * state_size)(*received[1][:-1])
    for n, members in enumerate(halves):
        last = slice(0 if n == 0 else -1, None)
        operands = (*received[n][last], messages[n], kvs[n], local_k, local_v) + ((start,) if n == 1 else ())
        column = functools.partial(lambda at, i: (0, at), n)
        results = [tokens_bf, tokens_bf, shape((heads, dim, dim), F32)]
        out_specs = [
            pl.BlockSpec((length, per * dim), column),
            pl.BlockSpec((length, per * dim), column),
            pl.BlockSpec((per, dim, dim), functools.partial(lambda at, i: (at, 0, 0), n)),
        ]
        if n == 0:
            results.append(shape((1, width), F32))
            out_specs.append(pl.BlockSpec((1, width), lambda i: (0, 0)))
        outs = call(
            functools.partial(final_kernel, members, dim, partners[last], n == 0), results, block, 5 * size + 4 * state_size,
            grid=(1,),
            in_specs=[WHOLE] * len(operands) + [pl.BlockSpec(memory_space=pl.ANY)] * len(outs),
            out_specs=out_specs,
            input_output_aliases={len(operands) + i: i for i in range(len(outs))},
        )(*operands, *outs)
        if n == 0:
            outs, grad_gain = outs[:3], outs[3]
    grad_k, grad_v, grad_state = outs
    return attended, grad_q, grad_k, grad_v, grad_state, grad_gain.reshape(width)


def solution(mesh):
    tokens = P("seq", "head")
    specs = (P("head", None, None), P("head"))
    return jax.shard_map(
        on_device,
        mesh=mesh,
        in_specs=(tokens,) * 4 + specs,
        out_specs=(tokens,) * 4 + specs,
        check_vma=False,
    )
```

```python
import functools

import jax
import jax.numpy as jnp
from jax import lax
from jax.experimental import pallas as pl
from jax.experimental.pallas import tpu as pltpu
from jax.sharding import PartitionSpec as P

EPS = 1e-05
F32 = jnp.float32
BF16 = jnp.bfloat16
VMEM = 16 * 2**20
PLANE = 4
EXTRA = 16
ROWS = 8
WHOLE = pl.BlockSpec(memory_space=pltpu.VMEM)
shape = jax.ShapeDtypeStruct


def dot(a, b, ca, cb):
    return lax.dot_general(a, b, (((ca,), (cb,)), ((), ())), preferred_element_type=F32)


def call(kernel, outs, flops, nbytes, **options):
    return pl.pallas_call(
        kernel,
        out_shape=outs,
        compiler_params=pltpu.CompilerParams(vmem_limit_bytes=VMEM),
        cost_estimate=pl.CostEstimate(flops=flops, bytes_accessed=nbytes, transcendentals=0),
        **options,
    )


def cols(h, dim):
    return slice(h * dim, (h + 1) * dim)


def causal(length, turned=False):
    rows = lax.broadcasted_iota(jnp.int32, (length, length), 1 if turned else 0)
    return rows >= lax.broadcasted_iota(jnp.int32, (length, length), 0 if turned else 1)


def state_kernel(halves, dim, *refs):
    n = len(halves)
    length = refs[0].shape[0] // 2
    for heads, kv_ref, wide_ref, narrow_ref in zip(halves, refs, refs[n:], refs[2 * n :]):
        for i in range(len(heads)):
            r = cols(i, dim)
            state = dot(kv_ref[:length, r], kv_ref[length:, r], 0, 0)
            wide_ref[r, :] = state
            narrow_ref[r, :] = state.astype(BF16)


def scores_kernel(halves, dim, q_ref, *refs):
    n = len(halves)
    local_ref, turned_ref = refs[n:]
    length = q_ref.shape[0]
    mask = causal(length)
    for heads, kv_ref in zip(halves, refs):
        for i, h in enumerate(heads):
            c, r = cols(h, dim), cols(i, dim)
            q = q_ref[:, c]
            turned_ref[c, :] = q.T
            scores = jnp.where(mask, dot(q, kv_ref[:length, r], 1, 1), 0.0).astype(BF16)
            local_ref[:, c] = dot(scores, kv_ref[length:, r], 1, 0)


def gathered(partners, parts, rows, reverse):
    mine = lax.axis_index("seq")
    total = None
    for partner, part in zip(partners, parts):
        top = 1 << (partner.bit_length() - 1)
        reached = (mine & top) == (0 if reverse else top)
        term = jnp.where(reached, part[rows, :].astype(F32), 0.0)
        total = term if total is None else total + term
    return total


def unnormed_kernel(heads, dim, partners, first, *refs):
    parts = refs[: len(partners)]
    refs = refs[len(partners) :]
    if not first:
        before, refs = refs[0], refs[1:]
    q_ref, local_ref, cot_ref, carried_ref, gain_ref, un_ref, prefix_ref, sums_ref = refs
    square = product = 0.0
    for i, h in enumerate(heads):
        c, r = cols(h, dim), cols(i, dim)
        prefix = (carried_ref[h] + gathered(partners, parts, r, False)).astype(BF16)
        prefix_ref[r, :] = prefix
        un = local_ref[:, c] + dot(q_ref[:, c], prefix, 1, 0)
        un_ref[:, r] = un
        square = square + un * un
        product = product + cot_ref[:, c].astype(F32) * gain_ref[:, c] * un
    square = jnp.sum(square.T, axis=0, keepdims=True)
    product = jnp.sum(product.T, axis=0, keepdims=True)
    row = lax.broadcasted_iota(jnp.int32, sums_ref.shape, 0)
    sums = jnp.where(row < ROWS // 2, square, product)
    sums_ref[...] = sums if first else sums + before[...]


def scales(sums_ref, other_ref, width, dim):
    sums = sums_ref[...] + other_ref[...]
    inverse = lax.rsqrt(sums[0:1, :] / width + EPS)
    factor = (sums[ROWS // 2 : ROWS // 2 + 1, :] * inverse) / width * inverse * inverse
    length = sums.shape[1]
    return [jnp.broadcast_to(row, (dim, length)).T for row in (inverse, factor)]


def norm_kernel(halves, dim, width, *refs):
    n = len(halves)
    sums_ref, other_ref = refs[:2]
    uns = refs[2 : 2 + n]
    cot_ref, gain_ref, q_ref = refs[2 + n : 5 + n]
    guns, messages, inverse_ref = refs[5 + n : 5 + 2 * n], refs[5 + 2 * n : 5 + 3 * n], refs[5 + 3 * n]
    inverse, factor = scales(sums_ref, other_ref, width, dim)
    inverse_ref[...] = inverse
    row = lax.broadcasted_iota(jnp.int32, (EXTRA, dim), 0)
    gains = jnp.zeros((EXTRA, dim), F32)
    for heads, un_ref, gun_ref, msg_ref in zip(halves, uns, guns, messages):
        for i, h in enumerate(heads):
            c, r = cols(h, dim), cols(i, dim)
            un = un_ref[:, r]
            cot = cot_ref[:, c].astype(F32)
            gun = (cot * gain_ref[:, c] * inverse - un * factor).astype(BF16)
            gun_ref[:, r] = gun
            msg_ref[r, :] = dot(q_ref[c, :], gun, 1, 0).astype(BF16)
            gains = jnp.where(row == h, jnp.sum(cot * (un * inverse), axis=0, keepdims=True), gains)
    messages[0][len(halves[0]) * dim :, :] = gains.astype(BF16)


def attended_kernel(halves, dim, *refs):
    n = len(halves)
    uns, guns, prefixes = refs[:n], refs[n : 2 * n], refs[2 * n : 3 * n]
    kvs = refs[3 * n : 4 * n]
    inverse_ref, gain_ref, att_ref, gq_ref = refs[4 * n :]
    inverse = inverse_ref[...]
    length = kvs[0].shape[0] // 2
    mask = causal(length)
    for heads, un_ref, gun_ref, prefix_ref, kv_ref in zip(halves, uns, guns, prefixes, kvs):
        for i, h in enumerate(heads):
            c, r = cols(h, dim), cols(i, dim)
            att_ref[:, c] = (gain_ref[:, c] * (un_ref[:, r] * inverse)).astype(BF16)
            gun = gun_ref[:, r]
            mixed = jnp.where(mask, dot(gun, kv_ref[length:, r], 1, 1), 0.0).astype(BF16)
            gq = dot(mixed, kv_ref[:length, r], 1, 0) + dot(gun, prefix_ref[r, :], 1, 1)
            gq_ref[:, c] = gq.astype(BF16)


def local_kernel(halves, dim, *refs):
    n = len(halves)
    guns, kvs = refs[:n], refs[n : 2 * n]
    q_ref, gk_ref, gv_ref = refs[2 * n :]
    length = q_ref.shape[0]
    mask = causal(length, True)
    for heads, gun_ref, kv_ref in zip(halves, guns, kvs):
        for i, h in enumerate(heads):
            c, r = cols(h, dim), cols(i, dim)
            q, k, gun = q_ref[:, c], kv_ref[:length, r], gun_ref[:, r]
            mixed = jnp.where(mask, dot(kv_ref[length:, r], gun, 1, 1), 0.0).astype(BF16)
            scores = jnp.where(mask, dot(k, q, 1, 1), 0.0).astype(BF16)
            gk_ref[:, c] = dot(mixed, q, 1, 0)
            gv_ref[:, c] = dot(scores, gun, 1, 0)


def final_kernel(heads, dim, partners, first, *refs):
    parts = refs[: len(partners)]
    message_ref, kv_ref, gk_ref, gv_ref = refs[len(partners) : len(partners) + 4]
    outs = refs[len(partners) + (4 if first else 7) :]
    gk_out, gv_out, state_out = outs[:3]
    length = kv_ref.shape[0] // 2
    for i, h in enumerate(heads):
        c, r = cols(h, dim), cols(i, dim)
        suffix = gathered(partners, parts, r, True).astype(BF16)
        gk = gk_ref[:, c] + dot(kv_ref[length:, r], suffix, 1, 1)
        gv = gv_ref[:, c] + dot(kv_ref[:length, r], suffix, 1, 0)
        gk_out[:, r] = gk.astype(BF16)
        gv_out[:, r] = gv.astype(BF16)
        state_out[i] = message_ref[r, :].astype(F32) + parts[-1][r, :].astype(F32)
    if first:
        tail = slice(len(heads) * dim, len(heads) * dim + EXTRA)
        gains = message_ref[tail, :].astype(F32) + parts[-1][tail, :].astype(F32)
        for h in range(outs[3].shape[1] // dim):
            outs[3][:, cols(h, dim)] = gains[h : h + 1, :]


def swap(message, count, partner):
    return lax.ppermute(message, "seq", [(i, i ^ partner) for i in range(count)])


def scan(messages, owns, count, beside):
    beside = dict(beside)
    received = [[swap(m, count, partner) for partner in range(1, PLANE)] for m in messages]
    partners = list(range(1, PLANE))
    distance = PLANE
    while distance < count:
        for n, parts in enumerate(received):
            got = parts if distance == PLANE else parts[-1:]
            if (n, distance) in beside:
                earlier = received[0]
                earlier[0], operands = lax.optimization_barrier((earlier[0], beside[n, distance][1:]))
                work = beside[n, distance][0](*operands)
                got, beside[n, distance] = lax.optimization_barrier((got, work))
                parts[-len(got) :] = got
            own = messages[n].astype(F32) if owns is None else owns[n]
            got = [part.astype(F32) for part in got]
            own = (own + got[0]) + (got[1] + got[2]) if distance == PLANE else own + got[0]
            messages[n] = own.astype(BF16)
            if owns is not None:
                owns[n] = own
        for n, parts in enumerate(received):
            parts.append(swap(messages[n], count, distance))
        partners.append(distance)
        distance *= 2
    return partners, messages, received, beside


def on_device(queries, key_rows, values, cotangent, carried_state, norm_gain):
    length, width = queries.shape
    heads, dim = carried_state.shape[:2]
    count = lax.axis_size("seq")
    head_count = lax.axis_size("head")
    assert count & (count - 1) == 0 and count > 2 * PLANE
    assert width == heads * dim and heads % 2 == 0
    total_width = width * head_count
    per = heads // 2
    assert heads <= EXTRA
    halves = [list(range(per)), list(range(per, heads))]
    gain = norm_gain.reshape(1, width)
    half_f32 = shape((length, per * dim), F32)
    half_bf = shape((length, per * dim), BF16)
    state_f32 = shape((per * dim, dim), F32)
    state_bf = shape((per * dim, dim), BF16)
    tokens_bf = shape((length, width), BF16)
    tokens_f32 = shape((length, width), F32)
    block = 2 * length * dim * dim * heads
    square = 2 * length * length * dim * heads
    size = length * width * 2
    state_size = heads * dim * dim * 2

    kvs = [
        jnp.concatenate([part[:, n * per * dim : (n + 1) * per * dim] for part in (key_rows, values)], axis=0)
        for n in range(len(halves))
    ]
    states = call(
        functools.partial(state_kernel, halves, dim),
        [state_f32] * 2 + [state_bf] * 2, block, 2 * size + state_size,
    )(*kvs)
    local = (call(
        functools.partial(scores_kernel, halves, dim),
        (tokens_f32, shape((width, length), BF16)), 2 * square, 5 * size,
    ), queries, *kvs)
    spot = (1, PLANE)
    partners, _, received, done = scan(list(states[2:]), list(states[:2]), count, {})
    local, turned = local[0](*local[1:])
    unnormed, prefixes, sums = [], [], ()
    for n, members in enumerate(halves):
        un, prefix, both = call(
            functools.partial(unnormed_kernel, members, dim, partners, n == 0),
            (half_f32, state_bf, shape((ROWS, length), F32)), block // 2, 3 * size + 4 * state_size,
        )(*received[n], *sums, queries, local, cotangent, carried_state, gain)
        unnormed.append(un)
        prefixes.append(prefix)
        sums = (both,)
    sums = sums[0]
    other = partner = sums
    for step in range(1, head_count):
        partner = lax.ppermute(partner, "head", [(i, (i + 1) % head_count) for i in range(head_count)])
        other = other + partner if step > 1 else partner

    *made, inverse = call(
        functools.partial(norm_kernel, halves, dim, total_width),
        (half_bf, half_bf, shape((per * dim + EXTRA, dim), BF16), state_bf, shape((length, dim), F32)),
        block, 6 * size,
    )(sums, other, *unnormed, cotangent, gain, turned)
    guns, messages = made[:2], made[2:]
    inner = (call(
        functools.partial(local_kernel, halves, dim), (tokens_f32, tokens_f32), 4 * square, 8 * size,
    ), *guns, *kvs, queries)
    attended, grad_q = call(
        functools.partial(attended_kernel, halves, dim),
        (tokens_bf, tokens_bf), 2 * square + block, 8 * size,
    )(*unnormed, *guns, *prefixes, *kvs, inverse, gain)
    partners, messages, received, done = scan(messages, None, count, {spot: inner})
    local_k, local_v = done[spot]

    outs = ()
    for n, members in enumerate(halves):
        operands = (*received[n], messages[n], kvs[n], local_k, local_v)
        column = functools.partial(lambda at, i: (0, at), n)
        results = [tokens_bf, tokens_bf, shape((heads, dim, dim), F32)]
        out_specs = [
            pl.BlockSpec((length, per * dim), column),
            pl.BlockSpec((length, per * dim), column),
            pl.BlockSpec((per, dim, dim), functools.partial(lambda at, i: (at, 0, 0), n)),
        ]
        if n == 0:
            results.append(shape((1, width), F32))
            out_specs.append(pl.BlockSpec((1, width), lambda i: (0, 0)))
        outs = call(
            functools.partial(final_kernel, members, dim, partners, n == 0), results, block, 5 * size + 4 * state_size,
            grid=(1,),
            in_specs=[WHOLE] * len(operands) + [pl.BlockSpec(memory_space=pl.ANY)] * len(outs),
            out_specs=out_specs,
            input_output_aliases={len(operands) + i: i for i in range(len(outs))},
        )(*operands, *outs)
        if n == 0:
            outs, grad_gain = outs[:3], outs[3]
    grad_k, grad_v, grad_state = outs
    return attended, grad_q, grad_k, grad_v, grad_state, grad_gain.reshape(width)


def solution(mesh):
    tokens = P("seq", "head")
    specs = (P("head", None, None), P("head"))
    return jax.shard_map(
        on_device,
        mesh=mesh,
        in_specs=(tokens,) * 4 + specs,
        out_specs=(tokens,) * 4 + specs,
        check_vma=False,
    )
```
